512 devices in a mesh: row: 8 (over x, core), col: 16 (over y_lo, z), layer: 4 (over y_hi).
Axes of the slice: x: 4, y: 8 (y_hi: 4, y_lo: 2; y = y_hi * 2 + y_lo), z: 8, core: 2. Of those that a mesh axis runs over, the one named last changes fastest.
Arguments:
- hamiltonian: bfloat16 [8192, 8192], P('row', ('col', 'layer')), as said below
- inv_root: bfloat16 [8192, 8192], P('row', 'col'), as said below
- h_pattern: int32 [32, 32], replicated, may hold values from 0 to 1, as said below
- z_pattern: int32 [32, 32], replicated, may hold values from 0 to 1, as said below
Outputs:
- transformed: bfloat16 [8192, 8192], P('row', ('col', 'layer'))
The draws below stay inside these ranges and needn't reach their ends.
Inputs may be any that keep to these rules, and one draw needn't show every extreme that they name: hamiltonian is symmetric. inv_root is symmetric. h_pattern is symmetric and every diagonal block is present. z_pattern is symmetric and every diagonal block is present.
All inputs are finite; a program needn't handle non-finite values.
Results may differ from the reference program's by a relative error of at most 0.005.
Values may be sent and summed in bfloat16 or wider, within the bound.
A program may use at most 64 MiB of HBM per device.

```python
import math
import jax
import jax.numpy as jnp

BLOCKS = 32
ORDER = 8192


def symmetric_noise(key):
    base = jax.random.truncated_normal(key, -4.0, 4.0, (ORDER, ORDER), jnp.float32)
    return (base + base.T) * 0.70710678


def block_pattern(key):
    reach = BLOCKS // 8
    scores = jax.random.randint(key, (BLOCKS, BLOCKS), 0, 100)
    paired = jnp.minimum(scores, scores.T)
    first = jnp.arange(BLOCKS, dtype=jnp.int32)[:, None]
    second = jnp.arange(BLOCKS, dtype=jnp.int32)[None, :]
    near = jnp.abs(first - second) <= reach
    return jnp.where(near | (paired < 30), 1, 0).astype(jnp.int32)


def draw_hamiltonian(key, part):
    noise = symmetric_noise(jax.random.fold_in(key, 11))
    return (noise * (1.6 / math.sqrt(ORDER))).astype(jnp.bfloat16)


def draw_inv_root(key, part):
    noise = symmetric_noise(jax.random.fold_in(key, 23))
    unit = jnp.eye(ORDER, dtype=jnp.float32)
    return (unit + noise * (0.632 / math.sqrt(ORDER))).astype(jnp.bfloat16)


def draw_h_pattern(key, part):
    return block_pattern(jax.random.fold_in(key, 37))


def draw_z_pattern(key, part):
    return block_pattern(jax.random.fold_in(key, 41))


def setup_inputs(seed: int = 0) -> dict:
    key_list = jax.random.split(jax.random.key(seed), 5)
    return {
        "hamiltonian": draw_hamiltonian(jax.random.fold_in(key_list[4], 71), 0),
        "inv_root": draw_inv_root(jax.random.fold_in(key_list[4], 71), 0),
        "h_pattern": draw_h_pattern(jax.random.fold_in(key_list[4], 71), 0),
        "z_pattern": draw_z_pattern(jax.random.fold_in(key_list[4], 71), 0),
    }


def apply_pattern(matrix, pattern):
    blocks = pattern.shape[0]
    size = matrix.shape[0] // blocks
    shaped = matrix.reshape(blocks, size, blocks, size)
    keep = (pattern > 0)[:, None, :, None]
    kept = jnp.where(keep, shaped, jnp.zeros_like(shaped))
    return kept.reshape(matrix.shape)


def reference(hamiltonian, inv_root, h_pattern, z_pattern):
    masked_hamiltonian = apply_pattern(hamiltonian, h_pattern)
    masked_root = apply_pattern(inv_root, z_pattern)
    product = jnp.dot(masked_hamiltonian, masked_root, preferred_element_type=jnp.float32).astype(jnp.bfloat16)
    transformed = jnp.dot(masked_root.T, product, preferred_element_type=jnp.float32)
    return transformed.astype(jnp.bfloat16)
```

```python
import functools
import jax
import jax.numpy as jnp
from jax import lax
from jax.experimental import pallas as pl
from jax.experimental.pallas import tpu as pltpu
from jax.sharding import PartitionSpec as P

BS = 256
BF = jnp.bfloat16
F32 = jnp.float32
MESH = pl.DeviceIdType.MESH

SRC = ((0, 1, 3, 5), (0, 2, 4, 6))
DST = ((1, 3, 5, 7), (2, 4, 6, 7))

UNITS = {"u0": (0, 128), "u1": (128, 256), "u2": (384, 256), "v": (0, 640), "u3": (640, 256), "u4": (896, 128)}


def body(hp, zp, h_ref, z_ref, o_ref, ht, z1, z2, y, pbuf, xbuf, rss, rsr, cpart, csend, crecv,
         hs, hr, z1s, z1r, z2s, z2r, ks, kr, rs_s, rs_r, ag_s, ag_r, fs, fr, cs, cr):
    row = lax.axis_index("row")
    col = lax.axis_index("col")
    layer = lax.axis_index("layer")
    x, c = row // 2, lax.rem(row, 2)
    y_lo, z = col // 8, lax.rem(col, 8)
    y_pos = layer * 2 + y_lo

    def at_z(d):
        return {"col": y_lo * 8 + lax.rem(z + d + 8, 8)}

    def at_y(d):
        t = lax.rem(y_pos + d + 8, 8)
        return {"col": lax.rem(t, 2) * 8 + z, "layer": t // 2}

    def at_x(d):
        return {"row": lax.rem(x + d + 4, 4) * 2 + c}

    zdev = (at_z(1), at_z(-1))
    ydev = (at_y(1), at_y(-1))
    xdev = (at_x(1), at_x(2), at_x(3))
    sib = {"row": x * 2 + 1 - c}

    barrier = pltpu.get_barrier_semaphore()
    for d in (*zdev, *ydev, *xdev, sib):
        pl.semaphore_signal(barrier, inc=1, device_id=d, device_id_type=MESH)

    pending = []

    def rcopy(src, dst, s, r, dev):
        return pltpu.make_async_remote_copy(
            src_ref=src, dst_ref=dst, send_sem=s, recv_sem=r, device_id=dev, device_id_type=MESH
        )

    def go(cp):
        cp.start()
        pending.append(cp)

    for i in range(4):
        p = hp[row * 4 + i, col * 2 + layer // 2]
        keep = jnp.where(p > 0, 1.0, 0.0).astype(F32)
        blk = h_ref[i * BS:(i + 1) * BS, :].astype(F32) * keep
        ht[0:128, i * BS:(i + 1) * BS] = blk.T.astype(BF)

    pl.semaphore_wait(barrier, 8)

    def h_copy(d, s, j):
        return rcopy(
            ht.at[pl.ds(SRC[d][s] * 128 + j * 32, 32)], ht.at[pl.ds(DST[d][s] * 128 + j * 32, 32)],
            hs.at[d, s, j], hr.at[d, s, j], zdev[d],
        )

    for j in range(4):
        for d in range(2):
            go(h_copy(d, 0, j))

    for i in range(4):
        for k in range(2):
            p = zp[row * 4 + i, col * 2 + k]
            keep = jnp.where(p > 0, 1.0, 0.0).astype(F32)
            blk = z_ref[i * BS:(i + 1) * BS, k * BS:(k + 1) * BS].astype(F32) * keep
            z1[y_lo, i * BS:(i + 1) * BS, k * BS:(k + 1) * BS] = blk.astype(BF)

    def z1_copy(d, who):
        part = z1.at[who, pl.ds(d * 512, 512)]
        return rcopy(part, part, z1s.at[d], z1r.at[d], ydev[d])

    for d in range(2):
        go(z1_copy(d, y_lo))
    z2[0] = z1[y_lo, :, pl.ds(pl.multiple_of(layer * 128, 128), 128)]

    def z2_copy(d, s, j):
        start, size = j * 256, 256
        if s == 3:
            start, size = start + d * 128, 128
        return rcopy(
            z2.at[SRC[d][s], pl.ds(start, size)], z2.at[DST[d][s], pl.ds(start, size)],
            z2s.at[d, s, j], z2r.at[d, s, j], zdev[d],
        )

    def h_arrive(s, j):
        for d in range(2):
            h_copy(d, s, j).wait_recv()
            if s < 2 or (s == 2 and j // 2 == d):
                go(h_copy(d, s + 1, j))

    def h_last(j):
        for d in range(2):
            h_copy(d, 3, j + 2 * d).wait_recv()

    def z2_start(js):
        for j in js:
            for d in range(2):
                go(z2_copy(d, 0, j))

    def z2_arrive(s, js):
        for j in js:
            for d in range(2):
                z2_copy(d, s, j).wait_recv()
                if s < 3:
                    go(z2_copy(d, s + 1, j))

    other = 1 - y_lo
    TASKS = (("u0", y_lo, 1), ("u1", y_lo, 1), ("u2", y_lo, 1), ("v", other, 1), ("u3", 0, 2), ("u4", 0, 2))

    def geometry(t):
        name, h, nh = TASKS[t]
        r0, n = UNITS[name]
        mine = pl.multiple_of(r0 + c * (n // 2), 16)
        theirs = pl.multiple_of(r0 + (1 - c) * (n // 2), 16)
        return h, nh, r0, n, mine, theirs

    def quarter(t, q):
        h, nh, r0, n, mine, theirs = geometry(t)
        return pl.multiple_of(mine + q * (n // 8), 16), n // 8

    def s1(t):
        h, nh, r0, n, mine, theirs = geometry(t)
        for k in range(nh):
            pbuf[h + k, r0:r0 + n] = jnp.dot(ht[r0:r0 + n, :], z1[h + k], preferred_element_type=F32)
        go(k_copy(t, theirs))

    def k_copy(t, start):
        h, nh, r0, n, mine, theirs = geometry(t)
        return rcopy(
            pbuf.at[pl.ds(h, nh), pl.ds(start, n // 2)], xbuf.at[pl.ds(h, nh), pl.ds(start, n // 2)],
            ks.at[t], kr.at[t], sib,
        )

    def rs_copy(t, d, q):
        h, nh = TASKS[t][1:]
        start, size = quarter(t, q)
        return rcopy(
            rss.at[pl.ds(h, nh), pl.ds(start, size)], rsr.at[d, pl.ds(h, nh), pl.ds(start, size)],
            rs_s.at[t, d], rs_r.at[t, d], xdev[d],
        )

    def ag_copy(t, d, q):
        h, nh = TASKS[t][1:]
        start, size = quarter(t, q)
        part = y.at[pl.ds(h, nh), pl.ds(start, size)]
        return rcopy(part, part, ag_s.at[t, d], ag_r.at[t, d], xdev[d])

    def f_copy(t, start):
        h, nh, r0, n, mine, theirs = geometry(t)
        part = y.at[pl.ds(h, nh), pl.ds(start, n // 2)]
        return rcopy(part, part, fs.at[t], fr.at[t], sib)

    def s2(t):
        h, nh, r0, n, mine, theirs = geometry(t)
        k_copy(t, mine).wait_recv()
        for k in range(nh):
            v = pbuf[h + k, pl.ds(mine, n // 2)] + xbuf[h + k, pl.ds(mine, n // 2)]
            pbuf[h + k, pl.ds(mine, n // 2)] = v
            rss[h + k, pl.ds(mine, n // 2)] = v.astype(BF)
        for d in (1, 0, 2):
            go(rs_copy(t, d, lax.rem(x + d + 1, 4)))

    def s3(t):
        h, nh = TASKS[t][1:]
        start, size = quarter(t, x)
        for d in range(3):
            rs_copy(t, d, x).wait_recv()
        for k in range(nh):
            v = pbuf[h + k, pl.ds(start, size)]
            for d in range(3):
                v = v + rsr[d, h + k, pl.ds(start, size)].astype(F32)
            y[h + k, pl.ds(start, size)] = v.astype(BF)
        for d in (1, 0, 2):
            go(ag_copy(t, d, x))

    def s4(t):
        h, nh, r0, n, mine, theirs = geometry(t)
        for d in range(3):
            ag_copy(t, d, lax.rem(x + 3 - d, 4)).wait_recv()
        go(f_copy(t, mine))

    def s5(t):
        h, nh, r0, n, mine, theirs = geometry(t)
        f_copy(t, theirs).wait_recv()

    U0, U1, U2, V, U3, U4 = range(6)
    s1(U0)
    h_arrive(0, 0)
    s2(U0)
    h_arrive(0, 1)
    h_arrive(0, 2)
    h_arrive(0, 3)
    s1(U1)
    s3(U0)
    h_arrive(1, 0)
    s2(U1)
    h_arrive(1, 1)
    h_arrive(1, 2)
    s4(U0)
    h_arrive(1, 3)
    s1(U2)
    s3(U1)
    h_arrive(2, 0)
    s2(U2)
    for d in range(2):
        z1_copy(d, other).wait_recv()
    s1(V)
    h_arrive(2, 1)
    s2(V)
    s4(U1)
    h_arrive(2, 2)
    h_arrive(2, 3)
    z2_start((0, 1))
    s1(U3)
    s3(U2)
    h_last(0)
    h_last(1)
    s2(U3)
    s1(U4)
    s3(V)
    s2(U4)
    s4(U2)
    z2_arrive(0, (0, 1))
    z2_start((2, 3))
    s3(U3)
    s4(V)
    s3(U4)
    z2_arrive(1, (0, 1))
    z2_arrive(0, (2, 3))
    s4(U3)
    s4(U4)
    for t in range(6):
        s5(t)

    def block_of(d):
        t = lax.rem(y_pos + d + 8, 8)
        return lax.rem(t, 2) * 4 + t // 2

    def c_chunk(j):
        rows = pl.ds(j * 256, 256)
        left = jnp.concatenate([z2[s, rows] for s in range(8)], axis=1)
        for h in range(2):
            part = jnp.dot(left, y[h], preferred_element_type=F32)
            for b in range(4):
                cpart[h * 4 + b, rows] = part[:, b * 128:(b + 1) * 128]

    def c_copy(d, t, j):
        start, size = j * 256, 256
        if t == 0:
            start, size = start + d * 128, 128
        return rcopy(
            csend.at[d, t, pl.ds(start, size)], crecv.at[d, t, pl.ds(start, size)],
            cs.at[d, t, j], cr.at[d, t, j], ydev[d],
        )

    def c_step(t, j):
        for d in range(2):
            b = block_of((4 - t) * (1 - 2 * d))
            mine = pl.ds(j * 256 + d * 128, 128)
            rest = pl.ds(j * 256 + (1 - d) * 128, 128)
            full = pl.ds(j * 256, 256)
            if t == 0:
                csend[d, t, mine] = cpart[b, mine].astype(BF)
            else:
                c_copy(d, t - 1, j).wait_recv()
                if t == 1:
                    csend[d, t, mine] = (cpart[b, mine] + crecv[d, 0, mine].astype(F32)).astype(BF)
                    csend[d, t, rest] = cpart[b, rest].astype(BF)
                else:
                    csend[d, t, full] = (cpart[b, full] + crecv[d, t - 1, full].astype(F32)).astype(BF)
            go(c_copy(d, t, j))

    def c_last(j):
        full = pl.ds(j * 256, 256)
        v = cpart[block_of(0), full]
        for d in range(2):
            c_copy(d, 3, j).wait_recv()
            v = v + crecv[d, 3, full].astype(F32)
        o_ref[full, :] = v.astype(BF)

    z2_arrive(2, (0, 1))
    z2_arrive(1, (2, 3))
    z2_arrive(3, (0, 1))
    c_chunk(0)
    c_step(0, 0)
    c_chunk(1)
    c_step(0, 1)
    z2_arrive(2, (2, 3))
    c_step(1, 0)
    c_step(1, 1)
    z2_arrive(3, (2, 3))
    c_chunk(2)
    c_step(0, 2)
    c_chunk(3)
    c_step(0, 3)
    c_step(2, 0)
    c_step(2, 1)
    c_step(1, 2)
    c_step(1, 3)
    c_step(3, 0)
    c_step(3, 1)
    c_step(2, 2)
    c_step(2, 3)
    c_last(0)
    c_last(1)
    c_step(3, 2)
    c_step(3, 3)
    c_last(2)
    c_last(3)
    for cp in pending:
        cp.wait_send()


def local(hamiltonian, inv_root, h_pattern, z_pattern):
    dma = pltpu.SemaphoreType.DMA
    smem = pl.BlockSpec(memory_space=pltpu.SMEM)
    vmem = pl.BlockSpec(memory_space=pltpu.VMEM)
    return pl.pallas_call(
        body,
        out_shape=jax.ShapeDtypeStruct((1024, 128), BF),
        in_specs=[smem, smem, vmem, vmem],
        out_specs=vmem,
        scratch_shapes=[
            pltpu.VMEM((1024, 1024), BF),
            pltpu.VMEM((2, 1024, 512), BF),
            pltpu.VMEM((8, 1024, 128), BF),
            pltpu.VMEM((2, 1024, 512), BF),
            pltpu.VMEM((2, 1024, 512), F32),
            pltpu.VMEM((2, 1024, 512), F32),
            pltpu.VMEM((2, 1024, 512), BF),
            pltpu.VMEM((3, 2, 1024, 512), BF),
            pltpu.VMEM((8, 1024, 128), F32),
            pltpu.VMEM((2, 4, 1024, 128), BF),
            pltpu.VMEM((2, 4, 1024, 128), BF),
            dma((2, 4, 4)), dma((2, 4, 4)),
            dma((2,)), dma((2,)),
            dma((2, 4, 4)), dma((2, 4, 4)),
            dma((6,)), dma((6,)),
            dma((6, 3)), dma((6, 3)),
            dma((6, 3)), dma((6, 3)),
            dma((6,)), dma((6,)),
            dma((2, 4, 4)), dma((2, 4, 4)),
        ],
        compiler_params=pltpu.CompilerParams(
            collective_id=0, has_side_effects=True, vmem_limit_bytes=56 * 2**20
        ),
        cost_estimate=pl.CostEstimate(flops=4 * 1024**3, bytes_accessed=3 * 2**19, transcendentals=0),
    )(h_pattern, z_pattern, hamiltonian, inv_root)


def solution(mesh):
    return jax.shard_map(
        local,
        mesh=mesh,
        in_specs=(P("row", ("col", "layer")), P("row", "col"), P(), P()),
        out_specs=P("row", ("col", "layer")),
        check_vma=False,
    )
```

```python
import functools
import jax
import jax.numpy as jnp
from jax import lax
from jax.experimental import pallas as pl
from jax.experimental.pallas import tpu as pltpu
from jax.sharding import PartitionSpec as P

BS = 256
BF = jnp.bfloat16
F32 = jnp.float32
MESH = pl.DeviceIdType.MESH

SRC = ((0, 1, 3, 5), (0, 2, 4, 6))
DST = ((1, 3, 5, 7), (2, 4, 6, 7))

TASKS = ((0, 128, 0, 2), (128, 256, 0, 2), (0, 384, 2, 1), (384, 256, 0, 3), (0, 640, 3, 1), (640, 256, 0, 4), (896, 128, 0, 4))


def body(hp, zp, h_hbm, z_hbm, o_hbm, h_ref, z_ref, o_ref, ht, z1, z2, y, pbuf, xbuf, rss, rsr, cpart, csend, crecv,
         io, oo, hs, hr, z1s, z1r, z2s, z2r, ks, kr, rs_s, rs_r, ag_s, ag_r, fs, fr, cs, cr):
    row = lax.axis_index("row")
    col = lax.axis_index("col")
    layer = lax.axis_index("layer")
    x, c = row // 2, lax.rem(row, 2)
    y_lo, z = col // 8, lax.rem(col, 8)
    y_pos = layer * 2 + y_lo

    def at_z(d):
        return {"col": y_lo * 8 + lax.rem(z + d + 8, 8)}

    def at_y(d):
        t = lax.rem(y_pos + d + 8, 8)
        return {"col": lax.rem(t, 2) * 8 + z, "layer": t // 2}

    def at_x(d):
        return {"row": lax.rem(x + d + 4, 4) * 2 + c}

    zdev = (at_z(1), at_z(-1))
    ydev = (at_y(1), at_y(-1))
    xdev = (at_x(1), at_x(2), at_x(3))
    sib = {"row": x * 2 + 1 - c}

    loads = [pltpu.make_async_copy(h_hbm, h_ref, io.at[0]), pltpu.make_async_copy(z_hbm, z_ref, io.at[1])]
    for cp in loads:
        cp.start()
    barrier = pltpu.get_barrier_semaphore()
    for d in (*zdev, *ydev, *xdev, sib):
        pl.semaphore_signal(barrier, inc=1, device_id=d, device_id_type=MESH)

    pending = []

    def rcopy(src, dst, s, r, dev):
        return pltpu.make_async_remote_copy(
            src_ref=src, dst_ref=dst, send_sem=s, recv_sem=r, device_id=dev, device_id_type=MESH
        )

    def go(cp):
        cp.start()
        pending.append(cp)

    loads[0].wait()
    for i in range(4):
        p = hp[row * 4 + i, col * 2 + layer // 2]
        keep = jnp.where(p > 0, 1.0, 0.0).astype(F32)
        blk = h_ref[i * BS:(i + 1) * BS, :].astype(F32) * keep
        ht[0:128, i * BS:(i + 1) * BS] = blk.T.astype(BF)

    pl.semaphore_wait(barrier, 8)

    def h_copy(d, s, j):
        j = j if d == 0 else 3 - j
        return rcopy(
            ht.at[pl.ds(SRC[d][s] * 128 + j * 32, 32)], ht.at[pl.ds(DST[d][s] * 128 + j * 32, 32)],
            hs.at[d, s, j], hr.at[d, s, j], zdev[d],
        )

    for j in range(4):
        for d in range(2):
            go(h_copy(d, 0, j))

    def z1_copy(k, d):
        rows = pl.ds(d * 512, 512)
        return rcopy(z1.at[k, rows], z1.at[2 + k, rows], z1s.at[k, d], z1r.at[k, d], ydev[d])

    loads[1].wait()
    for k in range(2):
        for i in range(4):
            p = zp[row * 4 + i, col * 2 + k]
            keep = jnp.where(p > 0, 1.0, 0.0).astype(F32)
            blk = z_ref[i * BS:(i + 1) * BS, k * BS:(k + 1) * BS].astype(F32) * keep
            z1[k, i * BS:(i + 1) * BS, :] = blk.astype(BF)
        for d in range(2):
            go(z1_copy(k, d))
    z2[0] = z1[layer // 2, :, pl.ds(pl.multiple_of(lax.rem(layer, 2) * 128, 128), 128)]

    def z2_copy(d, s, j):
        start, size = j * 256, 256
        if s == 3:
            start, size = start + d * 128, 128
        return rcopy(
            z2.at[SRC[d][s], pl.ds(start, size)], z2.at[DST[d][s], pl.ds(start, size)],
            z2s.at[d, s, j], z2r.at[d, s, j], zdev[d],
        )

    def h_arrive(s, j):
        for d in range(2):
            h_copy(d, s, j).wait_recv()
            if s < 2 or (s == 2 and j < 2):
                go(h_copy(d, s + 1, j))

    def h_last(j):
        for d in range(2):
            h_copy(d, 3, j).wait_recv()

    def z2_start(js):
        for j in js:
            for d in range(2):
                go(z2_copy(d, 0, j))

    def z2_arrive(s, js):
        for j in js:
            for d in range(2):
                z2_copy(d, s, j).wait_recv()
                if s < 3:
                    go(z2_copy(d, s + 1, j))

    def geometry(t):
        r0, n, h, nh = TASKS[t]
        mine = pl.multiple_of(r0 + c * (n // 2), 16)
        theirs = pl.multiple_of(r0 + (1 - c) * (n // 2), 16)
        return h, nh, r0, n, mine, theirs

    def quarter(t, q):
        h, nh, r0, n, mine, theirs = geometry(t)
        return pl.multiple_of(mine + q * (n // 8), 16), n // 8

    def s1(t):
        h, nh, r0, n, mine, theirs = geometry(t)
        for k in range(nh):
            pbuf[h + k, r0:r0 + n] = jnp.dot(ht[r0:r0 + n, :], z1[h + k], preferred_element_type=F32)
        go(k_copy(t, theirs))

    def k_copy(t, start):
        h, nh, r0, n, mine, theirs = geometry(t)
        return rcopy(
            pbuf.at[pl.ds(h, nh), pl.ds(start, n // 2)], xbuf.at[pl.ds(h, nh), pl.ds(start, n // 2)],
            ks.at[t], kr.at[t], sib,
        )

    def rs_copy(t, d, q):
        h, nh = TASKS[t][2:]
        start, size = quarter(t, q)
        return rcopy(
            rss.at[pl.ds(h, nh), pl.ds(start, size)], rsr.at[d, pl.ds(h, nh), pl.ds(start, size)],
            rs_s.at[t, d], rs_r.at[t, d], xdev[d],
        )

    def ag_copy(t, d, q):
        h, nh = TASKS[t][2:]
        start, size = quarter(t, q)
        part = y.at[pl.ds(h, nh), pl.ds(start, size)]
        return rcopy(part, part, ag_s.at[t, d], ag_r.at[t, d], xdev[d])

    def f_copy(t, start):
        h, nh, r0, n, mine, theirs = geometry(t)
        part = y.at[pl.ds(h, nh), pl.ds(start, n // 2)]
        return rcopy(part, part, fs.at[t], fr.at[t], sib)

    def s2(t):
        h, nh, r0, n, mine, theirs = geometry(t)
        k_copy(t, mine).wait_recv()
        for k in range(nh):
            v = pbuf[h + k, pl.ds(mine, n // 2)] + xbuf[h + k, pl.ds(mine, n // 2)]
            pbuf[h + k, pl.ds(mine, n // 2)] = v
            rss[h + k, pl.ds(mine, n // 2)] = v.astype(BF)
        for d in (1, 0, 2):
            go(rs_copy(t, d, lax.rem(x + d + 1, 4)))

    def s3(t):
        h, nh = TASKS[t][2:]
        start, size = quarter(t, x)
        for d in range(3):
            rs_copy(t, d, x).wait_recv()
        for k in range(nh):
            v = pbuf[h + k, pl.ds(start, size)]
            for d in range(3):
                v = v + rsr[d, h + k, pl.ds(start, size)].astype(F32)
            y[h + k, pl.ds(start, size)] = v.astype(BF)
        for d in (1, 0, 2):
            go(ag_copy(t, d, x))

    def s4(t):
        h, nh, r0, n, mine, theirs = geometry(t)
        for d in range(3):
            ag_copy(t, d, lax.rem(x + 3 - d, 4)).wait_recv()
        go(f_copy(t, mine))

    def s5(t):
        h, nh, r0, n, mine, theirs = geometry(t)
        f_copy(t, theirs).wait_recv()

    def z1_arrive(k):
        for d in range(2):
            z1_copy(k, d).wait_recv()

    s1(0)
    h_arrive(0, 0)
    s2(0)
    h_arrive(0, 1)
    h_arrive(0, 2)
    h_arrive(0, 3)
    s3(0)
    s1(1)
    z1_arrive(0)
    s1(2)
    h_arrive(1, 0)
    h_arrive(1, 1)
    s2(1)
    s2(2)
    h_arrive(1, 2)
    s4(0)
    h_arrive(1, 3)
    s1(3)
    z1_arrive(1)
    s1(4)
    h_arrive(2, 0)
    s3(1)
    h_arrive(2, 1)
    s2(3)
    s2(4)
    s3(2)
    h_arrive(2, 2)
    z2_start((0, 1, 2, 3,))
    h_arrive(2, 3)
    s1(5)
    h_last(0)
    s2(5)
    h_last(1)
    s1(6)
    s3(3)
    z2_arrive(0, (0,))
    s3(4)
    s2(6)
    z2_arrive(0, (1,))
    z2_arrive(0, (2,))
    z2_arrive(0, (3,))
    s4(1)
    s4(2)
    z2_arrive(1, (0,))
    s3(5)
    z2_arrive(1, (1,))
    s3(6)
    z2_arrive(1, (2,))
    z2_arrive(1, (3,))
    s4(3)
    s4(4)
    z2_arrive(2, (0,))
    z2_arrive(2, (1,))
    z2_arrive(2, (2,))
    z2_arrive(2, (3,))
    s4(5)
    s4(6)
    z2_arrive(3, (0,))
    z2_arrive(3, (1,))
    s5(0)
    s5(1)
    s5(2)
    s5(3)
    s5(4)
    s5(5)
    s5(6)

    def block_of(d):
        t = lax.rem(y_pos + d + 8, 8)
        return (d % 2) * 4 + t // 2

    def c_chunk(j):
        rows = pl.ds(j * 256, 256)
        left = jnp.concatenate([z2[s, rows] for s in range(8)], axis=1)
        for q in range(4):
            part = jnp.dot(left, y[q], preferred_element_type=F32)
            for b in range(2):
                cpart[q * 2 + b, rows] = part[:, b * 128:(b + 1) * 128]

    def c_copy(d, t, j):
        start, size = j * 256, 256
        if t in (0, 1, 4):
            start, size = start + (1 - d if t == 4 else d) * 128, 128
        slot = 1 if t == 4 else t
        return rcopy(
            csend.at[d, slot, pl.ds(start, size)], crecv.at[d, slot, pl.ds(start, size)],
            cs.at[d, t, j], cr.at[d, t, j], ydev[d],
        )

    def c_start(j):
        for d in range(2):
            for t, half in ((0, d), (4, 1 - d)):
                rows = pl.ds(j * 256 + half * 128, 128)
                hop = 4 if t == 0 else 3
                csend[d, t // 4, rows] = cpart[block_of(hop * (1 - 2 * d)), rows].astype(BF)
                go(c_copy(d, t, j))

    def c_step(t, j):
        for d in range(2):
            b = block_of((4 - t) * (1 - 2 * d))
            rows = pl.ds(j * 256 + d * 128, 128) if t == 1 else pl.ds(j * 256, 256)
            c_copy(d, t - 1, j).wait_recv()
            if t == 2:
                c_copy(d, 4, j).wait_recv()
            csend[d, t, rows] = (cpart[b, rows] + crecv[d, t - 1, rows].astype(F32)).astype(BF)
            go(c_copy(d, t, j))

    stores = []

    def c_last(j):
        full = pl.ds(j * 256, 256)
        v = cpart[block_of(0), full]
        for d in range(2):
            c_copy(d, 3, j).wait_recv()
            v = v + crecv[d, 3, full].astype(F32)
        o_ref[full, :] = v.astype(BF)
        cp = pltpu.make_async_copy(o_ref.at[full], o_hbm.at[full], oo.at[j])
        cp.start()
        stores.append(cp)

    c_chunk(0)
    c_start(0)
    c_chunk(1)
    c_start(1)
    z2_arrive(3, (2,))
    c_chunk(2)
    c_start(2)
    z2_arrive(3, (3,))
    c_chunk(3)
    c_start(3)
    c_step(1, 0)
    c_step(1, 1)
    c_step(1, 2)
    c_step(1, 3)
    c_step(2, 0)
    c_step(2, 1)
    c_step(2, 2)
    c_step(2, 3)
    c_step(3, 0)
    c_step(3, 1)
    c_step(3, 2)
    c_step(3, 3)
    c_last(0)
    c_last(1)
    c_last(2)
    c_last(3)
    for cp in stores:
        cp.wait()
    for cp in pending:
        cp.wait_send()


def local(hamiltonian, inv_root, h_pattern, z_pattern):
    dma = pltpu.SemaphoreType.DMA
    smem = pl.BlockSpec(memory_space=pltpu.SMEM)
    hbm = pl.BlockSpec(memory_space=pl.ANY)
    return pl.pallas_call(
        body,
        out_shape=jax.ShapeDtypeStruct((1024, 128), BF),
        in_specs=[smem, smem, hbm, hbm],
        out_specs=hbm,
        scratch_shapes=[
            pltpu.VMEM((1024, 128), BF),
            pltpu.VMEM((1024, 512), BF),
            pltpu.VMEM((1024, 128), BF),
            pltpu.VMEM((1024, 1024), BF),
            pltpu.VMEM((4, 1024, 256), BF),
            pltpu.VMEM((8, 1024, 128), BF),
            pltpu.VMEM((4, 1024, 256), BF),
            pltpu.VMEM((4, 1024, 256), F32),
            pltpu.VMEM((4, 1024, 256), F32),
            pltpu.VMEM((4, 1024, 256), BF),
            pltpu.VMEM((3, 4, 1024, 256), BF),
            pltpu.VMEM((8, 1024, 128), F32),
            pltpu.VMEM((2, 4, 1024, 128), BF),
            pltpu.VMEM((2, 4, 1024, 128), BF),
            dma((2,)), dma((4,)),
            dma((2, 4, 4)), dma((2, 4, 4)),
            dma((2, 2)), dma((2, 2)),
            dma((2, 4, 4)), dma((2, 4, 4)),
            dma((7,)), dma((7,)),
            dma((7, 3)), dma((7, 3)),
            dma((7, 3)), dma((7, 3)),
            dma((7,)), dma((7,)),
            dma((2, 5, 4)), dma((2, 5, 4)),
        ],
        compiler_params=pltpu.CompilerParams(
            collective_id=0, has_side_effects=True, vmem_limit_bytes=56 * 2**20
        ),
        cost_estimate=pl.CostEstimate(flops=4 * 1024**3, bytes_accessed=3 * 2**19, transcendentals=0),
    )(h_pattern, z_pattern, hamiltonian, inv_root)


def solution(mesh):
    return jax.shard_map(
        local,
        mesh=mesh,
        in_specs=(P("row", ("col", "layer")), P("row", "col"), P(), P()),
        out_specs=P("row", ("col", "layer")),
        check_vma=False,
    )
```

```python
import functools
import jax
import jax.numpy as jnp
from jax import lax
from jax.experimental import pallas as pl
from jax.experimental.pallas import tpu as pltpu
from jax.sharding import PartitionSpec as P

BS = 256
BF = jnp.bfloat16
F32 = jnp.float32
MESH = pl.DeviceIdType.MESH

SRC = ((0, 1, 3, 5), (0, 2, 4, 6))
DST = ((1, 3, 5, 7), (2, 4, 6, 7))

TASKS = ((0, 128, 0, 2), (128, 256, 0, 2), (0, 384, 2, 1), (384, 256, 0, 3), (0, 640, 3, 1), (640, 256, 0, 4), (896, 128, 0, 4))

RING = (1, 2, 3, 4)


def body(hp, zp, h_hbm, z_hbm, o_hbm, h_ref, z_ref, o_ref, ht, z1, z2, y, pbuf, xbuf, rss, rsr, cpart, csend, crecv,
         io, oo, hs, hr, z1s, z1r, z2s, z2r, ks, kr, rs_s, rs_r, ag_s, ag_r, fs, fr, cs, cr):
    row = lax.axis_index("row")
    col = lax.axis_index("col")
    layer = lax.axis_index("layer")
    x, c = row // 2, lax.rem(row, 2)
    y_lo, z = col // 8, lax.rem(col, 8)
    y_pos = layer * 2 + y_lo

    def at_z(d):
        return {"col": y_lo * 8 + lax.rem(z + d + 8, 8)}

    def at_y(d):
        t = lax.rem(y_pos + d + 8, 8)
        return {"col": lax.rem(t, 2) * 8 + z, "layer": t // 2}

    def at_x(d):
        return {"row": lax.rem(x + d + 4, 4) * 2 + c}

    zdev = (at_z(1), at_z(-1))
    ydev = (at_y(1), at_y(-1))
    xdev = (at_x(1), at_x(2), at_x(3))
    sib = {"row": x * 2 + 1 - c}

    loads = [pltpu.make_async_copy(h_hbm, h_ref, io.at[0]), pltpu.make_async_copy(z_hbm, z_ref, io.at[1])]
    for cp in loads:
        cp.start()
    barrier = pltpu.get_barrier_semaphore()
    for d in (*zdev, *ydev, *xdev, sib):
        pl.semaphore_signal(barrier, inc=1, device_id=d, device_id_type=MESH)

    def rcopy(src, dst, s, r, dev):
        return pltpu.make_async_remote_copy(
            src_ref=src, dst_ref=dst, send_sem=s, recv_sem=r, device_id=dev, device_id_type=MESH
        )

    def await_all(ref, sem):
        pltpu.make_async_copy(ref, ref, sem).wait()

    def go(cp):
        cp.start()

    loads[0].wait()
    for i in range(4):
        p = hp[row * 4 + i, col * 2 + layer // 2]
        keep = jnp.where(p > 0, 1.0, 0.0).astype(F32)
        blk = h_ref[i * BS:(i + 1) * BS, :].astype(F32) * keep
        ht[0:128, i * BS:(i + 1) * BS] = blk.T.astype(BF)

    pl.semaphore_wait(barrier, 8)

    def h_copy(d, s, j):
        j = j if d == 0 else 3 - j
        return rcopy(
            ht.at[pl.ds(SRC[d][s] * 128 + j * 32, 32)], ht.at[pl.ds(DST[d][s] * 128 + j * 32, 32)],
            hs.at[0], hr.at[d, s, j], zdev[d],
        )

    for j in range(4):
        for d in range(2):
            go(h_copy(d, 0, j))

    def z1_copy(k, d):
        rows = pl.ds(d * 512, 512)
        return rcopy(z1.at[k, rows], z1.at[2 + k, rows], z1s.at[0], z1r.at[k, d], ydev[d])

    loads[1].wait()
    for k in range(2):
        for i in range(4):
            p = zp[row * 4 + i, col * 2 + k]
            keep = jnp.where(p > 0, 1.0, 0.0).astype(F32)
            blk = z_ref[i * BS:(i + 1) * BS, k * BS:(k + 1) * BS].astype(F32) * keep
            z1[k, i * BS:(i + 1) * BS, :] = blk.astype(BF)
        for d in range(2):
            go(z1_copy(k, d))
    z2[0] = z1[layer // 2, :, pl.ds(pl.multiple_of(lax.rem(layer, 2) * 128, 128), 128)]

    def z2_copy(d, s, j):
        start, size = j * 256, 256
        if s == 3:
            start, size = start + d * 128, 128
        return rcopy(
            z2.at[SRC[d][s], pl.ds(start, size)], z2.at[DST[d][s], pl.ds(start, size)],
            z2s.at[0], z2r.at[d, s, j], zdev[d],
        )

    def h_arrive(s, j):
        for d in range(2):
            h_copy(d, s, j).wait_recv()
            if s < 2 or (s == 2 and j < 2):
                go(h_copy(d, s + 1, j))

    def h_last(j):
        for d in range(2):
            h_copy(d, 3, j).wait_recv()

    def z2_start(js):
        for j in js:
            for d in range(2):
                go(z2_copy(d, 0, j))

    def z2_arrive(s, js):
        for j in js:
            for d in range(2):
                z2_copy(d, s, j).wait_recv()
                if s < 3:
                    go(z2_copy(d, s + 1, j))

    def geometry(t):
        r0, n, h, nh = TASKS[t]
        mine = pl.multiple_of(r0 + c * (n // 2), 16)
        theirs = pl.multiple_of(r0 + (1 - c) * (n // 2), 16)
        return h, nh, r0, n, mine, theirs

    def quarter(t, q):
        h, nh, r0, n, mine, theirs = geometry(t)
        return pl.multiple_of(mine + q * (n // 8), 16), n // 8

    def s1(t):
        h, nh, r0, n, mine, theirs = geometry(t)
        for k in range(nh):
            pbuf[h + k, r0:r0 + n] = jnp.dot(ht[r0:r0 + n, :], z1[h + k], preferred_element_type=F32)
        go(k_copy(t, theirs))

    def k_copy(t, start):
        h, nh, r0, n, mine, theirs = geometry(t)
        return rcopy(
            pbuf.at[pl.ds(h, nh), pl.ds(start, n // 2)], xbuf.at[pl.ds(h, nh), pl.ds(start, n // 2)],
            ks.at[0], kr.at[t], sib,
        )

    def rs_copy(t, d, q):
        h, nh = TASKS[t][2:]
        start, size = quarter(t, q)
        return rcopy(
            rss.at[pl.ds(h, nh), pl.ds(start, size)], rsr.at[d, pl.ds(h, nh), pl.ds(start, size)],
            rs_s.at[0], rs_r.at[t, 0], xdev[d],
        )

    def ag_copy(t, d, q):
        h, nh = TASKS[t][2:]
        start, size = quarter(t, q)
        part = y.at[pl.ds(h, nh), pl.ds(start, size)]
        return rcopy(part, part, ag_s.at[0], ag_r.at[t, 0], xdev[d])

    def f_copy(t, start):
        h, nh, r0, n, mine, theirs = geometry(t)
        part = y.at[pl.ds(h, nh), pl.ds(start, n // 2)]
        return rcopy(part, part, fs.at[0], fr.at[t], sib)

    def s2(t):
        h, nh, r0, n, mine, theirs = geometry(t)
        k_copy(t, mine).wait_recv()
        for k in range(nh):
            v = pbuf[h + k, pl.ds(mine, n // 2)] + xbuf[h + k, pl.ds(mine, n // 2)]
            pbuf[h + k, pl.ds(mine, n // 2)] = v
            rss[h + k, pl.ds(mine, n // 2)] = v.astype(BF)
        if t in RING:
            for i in (0, 3, 1, 4):
                go(ring_rs(t, i, x + 2 if i % 3 == 0 else x + sign(i)))
            return
        for d in (1, 0, 2):
            go(rs_copy(t, d, lax.rem(x + d + 1, 4)))

    def sign(i):
        return 1 if i < 3 else -1

    def half_rows(t, q, second):
        start, size = quarter(t, lax.rem(q + 4, 4))
        low = size // 32 * 16
        return pl.ds(start + low, size - low) if second else pl.ds(start, low)

    def ring_rs(t, i, q):
        h, nh = TASKS[t][2:]
        rows = half_rows(t, q, (i % 3 == 1) == (i < 3))
        d = 0 if i < 3 else 2
        return rcopy(
            rss.at[pl.ds(h, nh), rows], rsr.at[d, pl.ds(h, nh), rows], rs_s.at[0], rs_r.at[t, {0: 1, 3: 2}.get(i, 0)], xdev[d]
        )

    def s6(t):
        h, nh = TASKS[t][2:]
        for i in (0, 3):
            q = x + sign(i)
            rows = half_rows(t, q, i == 3)
            ring_rs(t, i, q).wait_recv()
            for k in range(nh):
                v = pbuf[h + k, rows] + rsr[0 if i == 0 else 2, h + k, rows].astype(F32)
                rss[h + k, rows] = v.astype(BF)
            go(ring_rs(t, i + 2, q))

    def ring_ag(t, i, q):
        h, nh = TASKS[t][2:]
        start, size = quarter(t, lax.rem(q + 4, 4))
        rows = pl.ds(start, size) if i < 2 else half_rows(t, q, i == 3)
        part = y.at[pl.ds(h, nh), rows]
        return rcopy(part, part, ag_s.at[0], ag_r.at[t, {0: 1, 1: 2}.get(i, 0)], xdev[i % 2 * 2])

    def s7(t):
        ring_ag(t, 0, x - 1).wait_recv()
        go(ring_ag(t, 2, x - 1))
        ring_ag(t, 1, x + 1).wait_recv()
        go(ring_ag(t, 3, x + 1))

    def s3(t):
        h, nh = TASKS[t][2:]
        start, size = quarter(t, x)
        await_all(rsr.at[pl.ds(0, 2 if t in RING else 3), pl.ds(h, nh), pl.ds(start, size)], rs_r.at[t, 0])
        for k in range(nh):
            v = pbuf[h + k, pl.ds(start, size)]
            for d in (0, 2) if t in RING else (0, 1, 2):
                v = v + rsr[d, h + k, pl.ds(start, size)].astype(F32)
            y[h + k, pl.ds(start, size)] = v.astype(BF)
        if t in RING:
            for i in range(2):
                go(ring_ag(t, i, x))
            return
        for d in (1, 0, 2):
            go(ag_copy(t, d, x))

    def s4(t):
        h, nh, r0, n, mine, theirs = geometry(t)
        await_all(y.at[pl.ds(h, nh), pl.ds(mine, n // 8 * (1 if t in RING else 3))], ag_r.at[t, 0])
        go(f_copy(t, mine))

    def s5(t):
        h, nh, r0, n, mine, theirs = geometry(t)
        f_copy(t, theirs).wait_recv()

    def z1_arrive(k):
        for d in range(2):
            z1_copy(k, d).wait_recv()

    def z1_arrive(k):
        for d in range(2):
            z1_copy(k, d).wait_recv()

    s1(0)
    h_arrive(0, 0)
    s2(0)
    h_arrive(0, 1)
    h_arrive(0, 2)
    h_arrive(0, 3)
    s3(0)
    s1(1)
    z1_arrive(0)
    s1(2)
    h_arrive(1, 0)
    s2(1)
    h_arrive(1, 1)
    s2(2)
    h_arrive(1, 2)
    s4(0)
    h_arrive(1, 3)
    s1(3)
    s6(1)
    z1_arrive(1)
    s1(4)
    h_arrive(2, 0)
    s6(2)
    s2(3)
    h_arrive(2, 1)
    s2(4)
    h_arrive(2, 2)
    z2_start((0, 1, 2, 3,))
    s3(1)
    s3(2)
    h_arrive(2, 3)
    s1(5)
    s6(3)
    h_last(0)
    s2(5)
    s6(4)
    h_last(1)
    s1(6)
    s7(1)
    s7(2)
    z2_arrive(0, (0,))
    s3(3)
    s2(6)
    z2_arrive(0, (1,))
    s3(4)
    z2_arrive(0, (2,))
    z2_arrive(0, (3,))
    s4(1)
    s4(2)
    z2_arrive(1, (0,))
    s3(5)
    z2_arrive(1, (1,))
    s7(3)
    s7(4)
    s3(6)
    z2_arrive(1, (2,))
    z2_arrive(1, (3,))
    s4(3)
    s4(4)
    z2_arrive(2, (0,))
    z2_arrive(2, (1,))
    z2_arrive(2, (2,))
    z2_arrive(2, (3,))
    s4(5)
    s4(6)
    z2_arrive(3, (0,))
    z2_arrive(3, (1,))
    s5(0)
    s5(1)
    s5(2)
    s5(3)
    s5(4)
    s5(5)
    s5(6)

    def block_of(d):
        t = lax.rem(y_pos + d + 8, 8)
        return (d % 2) * 4 + t // 2

    def c_chunk(j):
        rows = pl.ds(j * 256, 256)
        left = jnp.concatenate([z2[s, rows] for s in range(8)], axis=1)
        for q in range(4):
            part = jnp.dot(left, y[q], preferred_element_type=F32)
            for b in range(2):
                cpart[q * 2 + b, rows] = part[:, b * 128:(b + 1) * 128]

    def c_copy(d, t, j):
        start, size = j * 256, 256
        if t in (0, 1, 4):
            start, size = start + (1 - d if t == 4 else d) * 128, 128
        slot = 1 if t == 4 else t
        return rcopy(
            csend.at[d, slot, pl.ds(start, size)], crecv.at[d, slot, pl.ds(start, size)],
            cs.at[0], cr.at[d, t, j], ydev[d],
        )

    def c_start(j):
        for d in range(2):
            for t, half in ((0, d), (4, 1 - d)):
                rows = pl.ds(j * 256 + half * 128, 128)
                hop = 4 if t == 0 else 3
                csend[d, t // 4, rows] = cpart[block_of(hop * (1 - 2 * d)), rows].astype(BF)
                go(c_copy(d, t, j))

    def c_step(t, j):
        for d in range(2):
            b = block_of((4 - t) * (1 - 2 * d))
            rows = pl.ds(j * 256 + d * 128, 128) if t == 1 else pl.ds(j * 256, 256)
            c_copy(d, t - 1, j).wait_recv()
            if t == 2:
                c_copy(d, 4, j).wait_recv()
            csend[d, t, rows] = (cpart[b, rows] + crecv[d, t - 1, rows].astype(F32)).astype(BF)
            go(c_copy(d, t, j))

    stores = []

    def c_last(j):
        full = pl.ds(j * 256, 256)
        v = cpart[block_of(0), full]
        for d in range(2):
            c_copy(d, 3, j).wait_recv()
            v = v + crecv[d, 3, full].astype(F32)
        o_ref[full, :] = v.astype(BF)
        cp = pltpu.make_async_copy(o_ref.at[full], o_hbm.at[full], oo.at[j])
        cp.start()
        stores.append(cp)

    c_chunk(0)
    c_start(0)
    c_chunk(1)
    c_start(1)
    z2_arrive(3, (2,))
    c_chunk(2)
    c_start(2)
    z2_arrive(3, (3,))
    c_chunk(3)
    c_start(3)
    c_step(1, 0)
    c_step(1, 1)
    c_step(1, 2)
    c_step(1, 3)
    c_step(2, 0)
    c_step(2, 1)
    c_step(2, 2)
    c_step(2, 3)
    c_step(3, 0)
    c_step(3, 1)
    c_step(3, 2)
    c_step(3, 3)
    c_last(0)
    c_last(1)
    c_last(2)
    c_last(3)
    for cp in stores:
        cp.wait()
    await_all(ht.at[pl.ds(0, 896)], hs.at[0])
    await_all(z1.at[pl.ds(0, 2)], z1s.at[0])
    await_all(z2.at[pl.ds(0, 7)], z2s.at[0])
    await_all(pbuf.at[:, pl.ds(0, 512)], ks.at[0])
    await_all(rss.at[:, pl.ds(0, 384)], rs_s.at[0])
    await_all(y.at[:, pl.ds(0, 384)], ag_s.at[0])
    await_all(y.at[:, pl.ds(0, 512)], fs.at[0])
    await_all(z2.at[pl.ds(0, 7)], cs.at[0])


def local(hamiltonian, inv_root, h_pattern, z_pattern):
    dma = pltpu.SemaphoreType.DMA
    smem = pl.BlockSpec(memory_space=pltpu.SMEM)
    hbm = pl.BlockSpec(memory_space=pl.ANY)
    return pl.pallas_call(
        body,
        out_shape=jax.ShapeDtypeStruct((1024, 128), BF),
        in_specs=[smem, smem, hbm, hbm],
        out_specs=hbm,
        scratch_shapes=[
            pltpu.VMEM((1024, 128), BF),
            pltpu.VMEM((1024, 512), BF),
            pltpu.VMEM((1024, 128), BF),
            pltpu.VMEM((1024, 1024), BF),
            pltpu.VMEM((4, 1024, 256), BF),
            pltpu.VMEM((8, 1024, 128), BF),
            pltpu.VMEM((4, 1024, 256), BF),
            pltpu.VMEM((4, 1024, 256), F32),
            pltpu.VMEM((4, 1024, 256), F32),
            pltpu.VMEM((4, 1024, 256), BF),
            pltpu.VMEM((3, 4, 1024, 256), BF),
            pltpu.VMEM((8, 1024, 128), F32),
            pltpu.VMEM((2, 4, 1024, 128), BF),
            pltpu.VMEM((2, 4, 1024, 128), BF),
            dma((2,)), dma((4,)),
            dma((1,)), dma((2, 4, 4)),
            dma((1,)), dma((2, 2)),
            dma((1,)), dma((2, 4, 4)),
            dma((1,)), dma((7,)),
            dma((1,)), dma((7, 3)),
            dma((1,)), dma((7, 3)),
            dma((1,)), dma((7,)),
            dma((1,)), dma((2, 5, 4)),
        ],
        compiler_params=pltpu.CompilerParams(
            collective_id=0, has_side_effects=True, vmem_limit_bytes=56 * 2**20
        ),
        cost_estimate=pl.CostEstimate(flops=4 * 1024**3, bytes_accessed=3 * 2**19, transcendentals=0),
    )(h_pattern, z_pattern, hamiltonian, inv_root)


def solution(mesh):
    return jax.shard_map(
        local,
        mesh=mesh,
        in_specs=(P("row", ("col", "layer")), P("row", "col"), P(), P()),
        out_specs=P("row", ("col", "layer")),
        check_vma=False,
    )
```

```python
import functools
import jax
import jax.numpy as jnp
from jax import lax
from jax.experimental import pallas as pl
from jax.experimental.pallas import tpu as pltpu
from jax.sharding import PartitionSpec as P

BS = 256
BF = jnp.bfloat16
F32 = jnp.float32
MESH = pl.DeviceIdType.MESH

SRC = ((0, 1, 3, 5), (0, 2, 4, 6))
DST = ((1, 3, 5, 7), (2, 4, 6, 7))

TASKS = ((0, 128, 0, 2), (128, 256, 0, 2), (0, 384, 2, 1), (384, 256, 0, 3), (0, 640, 3, 1), (640, 256, 0, 4), (896, 128, 0, 4))

RING = (1, 2, 3, 4)


def body(hp, zp, h_hbm, z_hbm, o_hbm, h_ref, z_ref, o_ref, ht, z1, z2, y, pbuf, xbuf, rss, rsr, cpart, csend, crecv,
         io, oo, hs, hr, z1s, z1r, z2s, z2r, ks, kr, rs_s, rs_r, ag_s, ag_r, fs, fr, cs, cr):
    row = lax.axis_index("row")
    col = lax.axis_index("col")
    layer = lax.axis_index("layer")
    x, c = row // 2, lax.rem(row, 2)
    y_lo, z = col // 8, lax.rem(col, 8)
    y_pos = layer * 2 + y_lo

    def at_z(d):
        return {"col": y_lo * 8 + lax.rem(z + d + 8, 8)}

    def at_y(d):
        t = lax.rem(y_pos + d + 8, 8)
        return {"col": lax.rem(t, 2) * 8 + z, "layer": t // 2}

    def at_x(d):
        return {"row": lax.rem(x + d + 4, 4) * 2 + c}

    zdev = (at_z(1), at_z(-1))
    ydev = (at_y(1), at_y(-1))
    xdev = (at_x(1), at_x(2), at_x(3))
    sib = {"row": x * 2 + 1 - c}

    loads = [pltpu.make_async_copy(h_hbm, h_ref, io.at[0]), pltpu.make_async_copy(z_hbm, z_ref, io.at[1])]
    for cp in loads:
        cp.start()
    barrier = pltpu.get_barrier_semaphore()
    for d in (*zdev, *ydev, *xdev, sib):
        pl.semaphore_signal(barrier, inc=1, device_id=d, device_id_type=MESH)

    def rcopy(src, dst, s, r, dev):
        return pltpu.make_async_remote_copy(
            src_ref=src, dst_ref=dst, send_sem=s, recv_sem=r, device_id=dev, device_id_type=MESH
        )

    def await_all(ref, sem):
        pltpu.make_async_copy(ref, ref, sem).wait()

    def go(cp):
        cp.start()

    loads[0].wait()
    for i in range(4):
        p = hp[row * 4 + i, col * 2 + layer // 2]
        keep = jnp.where(p > 0, 1.0, 0.0).astype(F32)
        blk = h_ref[i * BS:(i + 1) * BS, :].astype(F32) * keep
        ht[0:128, i * BS:(i + 1) * BS] = blk.T.astype(BF)

    pl.semaphore_wait(barrier, 8)

    def h_copy(d, s, j):
        k, j = j, j if d == 0 else 3 - j
        return rcopy(
            ht.at[pl.ds(SRC[d][s] * 128 + j * 32, 32)], ht.at[pl.ds(DST[d][s] * 128 + j * 32, 32)],
            hs.at[0], hr.at[s, k], zdev[d],
        )

    for j in range(4):
        for d in range(2):
            go(h_copy(d, 0, j))

    def z1_copy(k, d):
        rows = pl.ds(d * 512, 512)
        return rcopy(z1.at[k, rows], z1.at[2 + k, rows], z1s.at[0], z1r.at[k, d], ydev[d])

    loads[1].wait()
    for k in range(2):
        for i in range(4):
            p = zp[row * 4 + i, col * 2 + k]
            keep = jnp.where(p > 0, 1.0, 0.0).astype(F32)
            blk = z_ref[i * BS:(i + 1) * BS, k * BS:(k + 1) * BS].astype(F32) * keep
            z1[k, i * BS:(i + 1) * BS, :] = blk.astype(BF)
        for d in range(2):
            go(z1_copy(k, d))
    z2[0] = z1[layer // 2, :, pl.ds(pl.multiple_of(lax.rem(layer, 2) * 128, 128), 128)]

    def z2_copy(d, s, j):
        start, size = j * 256, 256
        if s == 3:
            start, size = start + d * 128, 128
        return rcopy(
            z2.at[SRC[d][s], pl.ds(start, size)], z2.at[DST[d][s], pl.ds(start, size)],
            z2s.at[0], z2r.at[s, j], zdev[d],
        )

    def h_arrive(s, j):
        await_all(ht.at[pl.ds(0, 64)], hr.at[s, j])
        for d in range(2):
            if s < 2 or (s == 2 and j < 2):
                go(h_copy(d, s + 1, j))

    def h_last(j):
        await_all(ht.at[pl.ds(0, 64)], hr.at[3, j])

    def z2_start(js):
        for j in js:
            for d in range(2):
                go(z2_copy(d, 0, j))

    def z2_arrive(s, js):
        for j in js:
            await_all(z2.at[0, pl.ds(0, 256 if s == 3 else 512)], z2r.at[s, j])
            for d in range(2):
                if s < 3:
                    go(z2_copy(d, s + 1, j))

    def geometry(t):
        r0, n, h, nh = TASKS[t]
        mine = pl.multiple_of(r0 + c * (n // 2), 16)
        theirs = pl.multiple_of(r0 + (1 - c) * (n // 2), 16)
        return h, nh, r0, n, mine, theirs

    def quarter(t, q):
        h, nh, r0, n, mine, theirs = geometry(t)
        return pl.multiple_of(mine + q * (n // 8), 16), n // 8

    def s1(t):
        h, nh, r0, n, mine, theirs = geometry(t)
        for k in range(nh):
            pbuf[h + k, r0:r0 + n] = jnp.dot(ht[r0:r0 + n, :], z1[h + k], preferred_element_type=F32)
        go(k_copy(t, theirs))

    def k_copy(t, start):
        h, nh, r0, n, mine, theirs = geometry(t)
        return rcopy(
            pbuf.at[pl.ds(h, nh), pl.ds(start, n // 2)], xbuf.at[pl.ds(h, nh), pl.ds(start, n // 2)],
            ks.at[0], kr.at[t], sib,
        )

    def rs_copy(t, d, q):
        h, nh = TASKS[t][2:]
        start, size = quarter(t, q)
        return rcopy(
            rss.at[pl.ds(h, nh), pl.ds(start, size)], rsr.at[d, pl.ds(h, nh), pl.ds(start, size)],
            rs_s.at[0], rs_r.at[t], xdev[d],
        )

    def ag_copy(t, d, q):
        h, nh = TASKS[t][2:]
        start, size = quarter(t, q)
        part = y.at[pl.ds(h, nh), pl.ds(start, size)]
        return rcopy(part, part, ag_s.at[0], ag_r.at[t], xdev[d])

    def f_copy(t, start):
        h, nh, r0, n, mine, theirs = geometry(t)
        part = y.at[pl.ds(h, nh), pl.ds(start, n // 2)]
        return rcopy(part, part, fs.at[0], fr.at[t], sib)

    def s2(t):
        h, nh, r0, n, mine, theirs = geometry(t)
        k_copy(t, mine).wait_recv()
        for k in range(nh):
            v = pbuf[h + k, pl.ds(mine, n // 2)] + xbuf[h + k, pl.ds(mine, n // 2)]
            pbuf[h + k, pl.ds(mine, n // 2)] = v
            rss[h + k, pl.ds(mine, n // 2)] = v.astype(BF)
        if t in RING:
            for i in (0, 3, 1, 4):
                go(ring_rs(t, i, x + 2 if i % 3 == 0 else x + sign(i)))
            return
        for d in (0, 2, 1):
            go(rs_copy(t, d, lax.rem(x + d + 1, 4)))

    def sign(i):
        return 1 if i < 3 else -1

    def half_rows(t, q, second):
        start, size = quarter(t, lax.rem(q + 4, 4))
        low = size // 32 * 16
        return pl.ds(start + low, size - low) if second else pl.ds(start, low)

    def ring_rs(t, i, q):
        h, nh = TASKS[t][2:]
        rows = half_rows(t, q, (i % 3 == 1) == (i < 3))
        d = 0 if i < 3 else 2
        return rcopy(
            rss.at[pl.ds(h, nh), rows], rsr.at[d, pl.ds(h, nh), rows], rs_s.at[0], rs_r.at[7 + t if i % 3 == 0 else t], xdev[d]
        )

    def s6(t):
        h, nh = TASKS[t][2:]
        await_all(rsr.at[0, pl.ds(h, nh), pl.ds(*quarter(t, x))], rs_r.at[7 + t])
        for i in (0, 3):
            q = x + sign(i)
            rows = half_rows(t, q, i == 3)
            for k in range(nh):
                v = pbuf[h + k, rows] + rsr[0 if i == 0 else 2, h + k, rows].astype(F32)
                rss[h + k, rows] = v.astype(BF)
            go(ring_rs(t, i + 2, q))

    def ring_ag(t, i, q):
        h, nh = TASKS[t][2:]
        start, size = quarter(t, lax.rem(q + 4, 4))
        rows = pl.ds(start, size) if i < 2 else half_rows(t, q, i == 3)
        part = y.at[pl.ds(h, nh), rows]
        return rcopy(part, part, ag_s.at[0], ag_r.at[7 + t if i < 2 else t], xdev[i % 2 * 2])

    def s7(t):
        h, nh, r0, n, mine, theirs = geometry(t)
        await_all(y.at[pl.ds(h, nh), pl.ds(mine, n // 4)], ag_r.at[7 + t])
        go(ring_ag(t, 2, x - 1))
        go(ring_ag(t, 3, x + 1))

    def s3(t):
        h, nh = TASKS[t][2:]
        start, size = quarter(t, x)
        await_all(rsr.at[pl.ds(0, 2 if t in RING else 3), pl.ds(h, nh), pl.ds(start, size)], rs_r.at[t])
        for k in range(nh):
            v = pbuf[h + k, pl.ds(start, size)]
            for d in (0, 2) if t in RING else (0, 1, 2):
                v = v + rsr[d, h + k, pl.ds(start, size)].astype(F32)
            y[h + k, pl.ds(start, size)] = v.astype(BF)
        if t in RING:
            for i in range(2):
                go(ring_ag(t, i, x))
            return
        for d in (0, 2, 1):
            go(ag_copy(t, d, x))

    def s4(t):
        h, nh, r0, n, mine, theirs = geometry(t)
        await_all(y.at[pl.ds(h, nh), pl.ds(mine, n // 8 * (1 if t in RING else 3))], ag_r.at[t])
        go(f_copy(t, mine))

    def s5(t):
        h, nh, r0, n, mine, theirs = geometry(t)
        f_copy(t, theirs).wait_recv()

    def z1_arrive(k):
        for d in range(2):
            z1_copy(k, d).wait_recv()

    def z1_arrive(k):
        for d in range(2):
            z1_copy(k, d).wait_recv()

    s1(0)
    h_arrive(0, 0)
    s2(0)
    h_arrive(0, 1)
    h_arrive(0, 2)
    h_arrive(0, 3)
    s3(0)
    s1(1)
    z1_arrive(0)
    s1(2)
    h_arrive(1, 0)
    s2(1)
    h_arrive(1, 1)
    s2(2)
    h_arrive(1, 2)
    s4(0)
    h_arrive(1, 3)
    s1(3)
    s6(1)
    z1_arrive(1)
    s1(4)
    h_arrive(2, 0)
    s6(2)
    s2(3)
    h_arrive(2, 1)
    s2(4)
    h_arrive(2, 2)
    z2_start((0, 1, 2, 3,))
    s3(1)
    s3(2)
    h_arrive(2, 3)
    s1(5)
    s6(3)
    h_last(0)
    s2(5)
    s6(4)
    h_last(1)
    s1(6)
    s7(1)
    s7(2)
    z2_arrive(0, (0,))
    s3(3)
    s2(6)
    z2_arrive(0, (1,))
    s3(4)
    z2_arrive(0, (2,))
    s3(5)
    z2_arrive(0, (3,))
    s4(1)
    s4(2)
    z2_arrive(1, (0,))
    s7(3)
    s7(4)
    s3(6)
    z2_arrive(1, (1,))
    z2_arrive(1, (2,))
    z2_arrive(1, (3,))
    s4(5)
    z2_arrive(2, (0,))
    z2_arrive(2, (1,))
    s4(3)
    s4(4)
    s4(6)
    z2_arrive(2, (2,))
    z2_arrive(2, (3,))
    z2_arrive(3, (0,))
    z2_arrive(3, (1,))
    s5(0)
    s5(1)
    s5(2)
    s5(3)
    s5(4)
    s5(5)
    s5(6)

    def block_of(d):
        t = lax.rem(y_pos + d + 8, 8)
        return (d % 2) * 4 + t // 2

    def c_chunk(j):
        rows = pl.ds(j * 256, 256)
        left = jnp.concatenate([z2[s, rows] for s in range(8)], axis=1)
        for q in range(4):
            part = jnp.dot(left, y[q], preferred_element_type=F32)
            for b in range(2):
                cpart[q * 2 + b, rows] = part[:, b * 128:(b + 1) * 128]

    def c_copy(d, t, j):
        start, size = j * 256, 256
        if t in (0, 1, 4):
            start, size = start + (1 - d if t == 4 else d) * 128, 128
        slot = 1 if t == 4 else t
        return rcopy(
            csend.at[d, slot, pl.ds(start, size)], crecv.at[d, slot, pl.ds(start, size)],
            cs.at[0], cr.at[t, j], ydev[d],
        )

    def c_start(j):
        for d in range(2):
            for t, half in ((0, d), (4, 1 - d)):
                rows = pl.ds(j * 256 + half * 128, 128)
                hop = 4 if t == 0 else 3
                csend[d, t // 4, rows] = cpart[block_of(hop * (1 - 2 * d)), rows].astype(BF)
                go(c_copy(d, t, j))

    def c_wait(t, j):
        await_all(crecv.at[0, 0, pl.ds(0, 512 if t in (2, 3) else 256)], cr.at[t, j])

    def c_step(t, j):
        c_wait(t - 1, j)
        if t == 2:
            c_wait(4, j)
        for d in range(2):
            b = block_of((4 - t) * (1 - 2 * d))
            rows = pl.ds(j * 256 + d * 128, 128) if t == 1 else pl.ds(j * 256, 256)
            csend[d, t, rows] = (cpart[b, rows] + crecv[d, t - 1, rows].astype(F32)).astype(BF)
            go(c_copy(d, t, j))

    stores = []

    def c_last(j):
        full = pl.ds(j * 256, 256)
        v = cpart[block_of(0), full]
        c_wait(3, j)
        for d in range(2):
            v = v + crecv[d, 3, full].astype(F32)
        o_ref[full, :] = v.astype(BF)
        cp = pltpu.make_async_copy(o_ref.at[full], o_hbm.at[full], oo.at[j])
        cp.start()
        stores.append(cp)

    c_chunk(0)
    c_start(0)
    c_chunk(1)
    c_start(1)
    z2_arrive(3, (2,))
    c_chunk(2)
    c_start(2)
    z2_arrive(3, (3,))
    c_chunk(3)
    c_start(3)
    c_step(1, 0)
    c_step(1, 1)
    c_step(1, 2)
    c_step(1, 3)
    c_step(2, 0)
    c_step(2, 1)
    c_step(2, 2)
    c_step(2, 3)
    c_step(3, 0)
    c_step(3, 1)
    c_step(3, 2)
    c_step(3, 3)
    c_last(0)
    c_last(1)
    c_last(2)
    c_last(3)
    for cp in stores:
        cp.wait()
    await_all(ht.at[pl.ds(0, 896)], hs.at[0])
    await_all(z1.at[pl.ds(0, 2)], z1s.at[0])
    await_all(z2.at[pl.ds(0, 7)], z2s.at[0])
    await_all(pbuf.at[:, pl.ds(0, 512)], ks.at[0])
    await_all(rss.at[:, pl.ds(0, 384)], rs_s.at[0])
    await_all(y.at[:, pl.ds(0, 384)], ag_s.at[0])
    await_all(y.at[:, pl.ds(0, 512)], fs.at[0])
    await_all(z2.at[pl.ds(0, 7)], cs.at[0])


def local(hamiltonian, inv_root, h_pattern, z_pattern):
    dma = pltpu.SemaphoreType.DMA
    smem = pl.BlockSpec(memory_space=pltpu.SMEM)
    hbm = pl.BlockSpec(memory_space=pl.ANY)
    return pl.pallas_call(
        body,
        out_shape=jax.ShapeDtypeStruct((1024, 128), BF),
        in_specs=[smem, smem, hbm, hbm],
        out_specs=hbm,
        scratch_shapes=[
            pltpu.VMEM((1024, 128), BF),
            pltpu.VMEM((1024, 512), BF),
            pltpu.VMEM((1024, 128), BF),
            pltpu.VMEM((1024, 1024), BF),
            pltpu.VMEM((4, 1024, 256), BF),
            pltpu.VMEM((8, 1024, 128), BF),
            pltpu.VMEM((4, 1024, 256), BF),
            pltpu.VMEM((4, 1024, 256), F32),
            pltpu.VMEM((4, 1024, 256), F32),
            pltpu.VMEM((4, 1024, 256), BF),
            pltpu.VMEM((3, 4, 1024, 256), BF),
            pltpu.VMEM((8, 1024, 128), F32),
            pltpu.VMEM((2, 4, 1024, 128), BF),
            pltpu.VMEM((2, 4, 1024, 128), BF),
            dma((2,)), dma((4,)),
            dma((1,)), dma((4, 4)),
            dma((1,)), dma((2, 2)),
            dma((1,)), dma((4, 4)),
            dma((1,)), dma((7,)),
            dma((1,)), dma((12,)),
            dma((1,)), dma((12,)),
            dma((1,)), dma((7,)),
            dma((1,)), dma((5, 4)),
        ],
        compiler_params=pltpu.CompilerParams(
            collective_id=0, has_side_effects=True, vmem_limit_bytes=56 * 2**20
        ),
        cost_estimate=pl.CostEstimate(flops=4 * 1024**3, bytes_accessed=3 * 2**19, transcendentals=0),
    )(h_pattern, z_pattern, hamiltonian, inv_root)


def solution(mesh):
    return jax.shard_map(
        local,
        mesh=mesh,
        in_specs=(P("row", ("col", "layer")), P("row", "col"), P(), P()),
        out_specs=P("row", ("col", "layer")),
        check_vma=False,
    )
```

```python
import functools
import jax
import jax.numpy as jnp
from jax import lax
from jax.experimental import pallas as pl
from jax.experimental.pallas import tpu as pltpu
from jax.sharding import PartitionSpec as P

BS = 256
BF = jnp.bfloat16
F32 = jnp.float32
MESH = pl.DeviceIdType.MESH

SRC = ((0, 1, 3, 5), (0, 2, 4, 6))
DST = ((1, 3, 5, 7), (2, 4, 6, 7))

TASKS = (
    (0, 128, 0, 4), (128, 256, 0, 4), (0, 384, 4, 2), (0, 384, 6, 1),
    (384, 256, 0, 7), (0, 640, 7, 1), (640, 256, 0, 8), (896, 128, 0, 8),
)

RING = (4, 5)


def body(hp, zp, h_hbm, z_hbm, o_hbm, h_ref, z_ref, o_ref, ht, z1, z2, y, pbuf, xbuf, rss, rsr, cpart, csend, crecv,
         io, oo, hs, hr, z1s, z1r, z2s, z2r, ks, kr, rs_s, rs_r, ag_s, ag_r, fs, fr, cs, cr):
    row = lax.axis_index("row")
    col = lax.axis_index("col")
    layer = lax.axis_index("layer")
    x, c = row // 2, lax.rem(row, 2)
    y_lo, z = col // 8, lax.rem(col, 8)
    y_pos = layer * 2 + y_lo

    def at_z(d):
        return {"col": y_lo * 8 + lax.rem(z + d + 8, 8)}

    def at_y(d):
        t = lax.rem(y_pos + d + 8, 8)
        return {"col": lax.rem(t, 2) * 8 + z, "layer": t // 2}

    def at_x(d):
        return {"row": lax.rem(x + d + 4, 4) * 2 + c}

    zdev = (at_z(1), at_z(-1))
    ydev = (at_y(1), at_y(-1))
    xdev = (at_x(1), at_x(2), at_x(3))
    sib = {"row": x * 2 + 1 - c}

    loads = [pltpu.make_async_copy(h_hbm, h_ref, io.at[0]), pltpu.make_async_copy(z_hbm, z_ref, io.at[1])]
    for cp in loads:
        cp.start()
    barrier = pltpu.get_barrier_semaphore()
    for d in (*zdev, *ydev, *xdev, sib):
        pl.semaphore_signal(barrier, inc=1, device_id=d, device_id_type=MESH)

    def rcopy(src, dst, s, r, dev):
        return pltpu.make_async_remote_copy(
            src_ref=src, dst_ref=dst, send_sem=s, recv_sem=r, device_id=dev, device_id_type=MESH
        )

    def await_all(ref, sem):
        pltpu.make_async_copy(ref, ref, sem).wait()

    def go(cp):
        cp.start()

    loads[0].wait()
    for i in range(4):
        p = hp[row * 4 + i, col * 2 + layer // 2]
        keep = jnp.where(p > 0, 1.0, 0.0).astype(F32)
        blk = h_ref[i * BS:(i + 1) * BS, :].astype(F32) * keep
        ht[0:128, i * BS:(i + 1) * BS] = blk.T.astype(BF)

    pl.semaphore_wait(barrier, 8)

    def h_copy(d, s, j):
        k, j = j, j if d == 0 else 3 - j
        return rcopy(
            ht.at[pl.ds(SRC[d][s] * 128 + j * 32, 32)], ht.at[pl.ds(DST[d][s] * 128 + j * 32, 32)],
            hs.at[0], hr.at[s, k], zdev[d],
        )

    for j in range(4):
        for d in range(2):
            go(h_copy(d, 0, j))

    def z1_copy(k, d):
        rows = pl.ds(d * 512, 512)
        return rcopy(z1.at[k, rows], z1.at[4 + k, rows], z1s.at[0], z1r.at[k, d], ydev[d])

    loads[1].wait()
    for k in range(2):
        for i in range(4):
            p = zp[row * 4 + i, col * 2 + k]
            keep = jnp.where(p > 0, 1.0, 0.0).astype(F32)
            blk = z_ref[i * BS:(i + 1) * BS, k * BS:(k + 1) * BS].astype(F32) * keep
            for m in range(2):
                z1[2 * k + m, i * BS:(i + 1) * BS, :] = blk[:, m * 128:(m + 1) * 128].astype(BF)
        for m in range(2):
            for d in range(2):
                go(z1_copy(2 * k + m, d))
    z2[0] = z1[layer]

    def z2_copy(d, s, j):
        start, size = j * 256, 256
        if s == 3:
            start, size = start + d * 128, 128
        return rcopy(
            z2.at[SRC[d][s], pl.ds(start, size)], z2.at[DST[d][s], pl.ds(start, size)],
            z2s.at[0], z2r.at[s, j], zdev[d],
        )

    def h_arrive(s, j):
        await_all(ht.at[pl.ds(0, 64)], hr.at[s, j])
        for d in range(2):
            if s < 2 or (s == 2 and j < 2):
                go(h_copy(d, s + 1, j))

    def h_last(j):
        await_all(ht.at[pl.ds(0, 64)], hr.at[3, j])

    def z2_start(js):
        for j in js:
            for d in range(2):
                go(z2_copy(d, 0, j))

    def z2_arrive(s, js):
        for j in js:
            await_all(z2.at[0, pl.ds(0, 256 if s == 3 else 512)], z2r.at[s, j])
            for d in range(2):
                if s < 3:
                    go(z2_copy(d, s + 1, j))

    def geometry(t):
        r0, n, h, nh = TASKS[t]
        mine = pl.multiple_of(r0 + c * (n // 2), 16)
        theirs = pl.multiple_of(r0 + (1 - c) * (n // 2), 16)
        return h, nh, r0, n, mine, theirs

    def quarter(t, q):
        h, nh, r0, n, mine, theirs = geometry(t)
        return pl.multiple_of(mine + q * (n // 8), 16), n // 8

    def s1(t):
        h, nh, r0, n, mine, theirs = geometry(t)
        for k in range(0, nh, 2):
            w = min(2, nh - k)
            right = z1[h + k] if w == 1 else jnp.concatenate([z1[h + k], z1[h + k + 1]], axis=1)
            part = jnp.dot(ht[r0:r0 + n, :], right, preferred_element_type=F32)
            for m in range(w):
                pbuf[h + k + m, r0:r0 + n] = part[:, m * 128:(m + 1) * 128]
        go(k_copy(t, theirs))

    def k_copy(t, start):
        h, nh, r0, n, mine, theirs = geometry(t)
        return rcopy(
            pbuf.at[pl.ds(h, nh), pl.ds(start, n // 2)], xbuf.at[pl.ds(h, nh), pl.ds(start, n // 2)],
            ks.at[0], kr.at[t], sib,
        )

    def rs_copy(t, d, q):
        h, nh = TASKS[t][2:]
        start, size = quarter(t, q)
        return rcopy(
            rss.at[pl.ds(h, nh), pl.ds(start, size)], rsr.at[d, pl.ds(h, nh), pl.ds(start, size)],
            rs_s.at[0], rs_r.at[t], xdev[d],
        )

    def ag_copy(t, d, q):
        h, nh = TASKS[t][2:]
        start, size = quarter(t, q)
        part = y.at[pl.ds(h, nh), pl.ds(start, size)]
        return rcopy(part, part, ag_s.at[0], ag_r.at[t], xdev[d])

    def f_copy(t, start):
        h, nh, r0, n, mine, theirs = geometry(t)
        part = y.at[pl.ds(h, nh), pl.ds(start, n // 2)]
        return rcopy(part, part, fs.at[0], fr.at[t], sib)

    def s2(t):
        h, nh, r0, n, mine, theirs = geometry(t)
        k_copy(t, mine).wait_recv()
        for k in range(nh):
            v = pbuf[h + k, pl.ds(mine, n // 2)] + xbuf[h + k, pl.ds(mine, n // 2)]
            pbuf[h + k, pl.ds(mine, n // 2)] = v
            rss[h + k, pl.ds(mine, n // 2)] = v.astype(BF)
        if t in RING:
            for i in (0, 3, 1, 4):
                go(ring_rs(t, i, x + 2 if i % 3 == 0 else x + sign(i)))
            return
        for d in (0, 2, 1):
            go(rs_copy(t, d, lax.rem(x + d + 1, 4)))

    def sign(i):
        return 1 if i < 3 else -1

    def half_rows(t, q, second):
        start, size = quarter(t, lax.rem(q + 4, 4))
        low = size // 32 * 16
        return pl.ds(start + low, size - low) if second else pl.ds(start, low)

    def ring_rs(t, i, q):
        h, nh = TASKS[t][2:]
        rows = half_rows(t, q, (i % 3 == 1) == (i < 3))
        d = 0 if i < 3 else 2
        return rcopy(
            rss.at[pl.ds(h, nh), rows], rsr.at[d, pl.ds(h, nh), rows], rs_s.at[0], rs_r.at[8 + t if i % 3 == 0 else t], xdev[d]
        )

    def s6(t):
        h, nh = TASKS[t][2:]
        await_all(rsr.at[0, pl.ds(h, nh), pl.ds(*quarter(t, x))], rs_r.at[8 + t])
        for i in (0, 3):
            q = x + sign(i)
            rows = half_rows(t, q, i == 3)
            for k in range(nh):
                v = pbuf[h + k, rows] + rsr[0 if i == 0 else 2, h + k, rows].astype(F32)
                rss[h + k, rows] = v.astype(BF)
            go(ring_rs(t, i + 2, q))

    def ring_ag(t, i, q):
        h, nh = TASKS[t][2:]
        start, size = quarter(t, lax.rem(q + 4, 4))
        rows = pl.ds(start, size) if i < 2 else half_rows(t, q, i == 3)
        part = y.at[pl.ds(h, nh), rows]
        return rcopy(part, part, ag_s.at[0], ag_r.at[8 + t if i < 2 else t], xdev[i % 2 * 2])

    def s7(t):
        h, nh, r0, n, mine, theirs = geometry(t)
        await_all(y.at[pl.ds(h, nh), pl.ds(mine, n // 4)], ag_r.at[8 + t])
        go(ring_ag(t, 2, x - 1))
        go(ring_ag(t, 3, x + 1))

    def s3(t):
        h, nh = TASKS[t][2:]
        start, size = quarter(t, x)
        await_all(rsr.at[pl.ds(0, 2 if t in RING else 3), pl.ds(h, nh), pl.ds(start, size)], rs_r.at[t])
        for k in range(nh):
            v = pbuf[h + k, pl.ds(start, size)]
            for d in (0, 2) if t in RING else (0, 1, 2):
                v = v + rsr[d, h + k, pl.ds(start, size)].astype(F32)
            y[h + k, pl.ds(start, size)] = v.astype(BF)
        if t in RING:
            for i in range(2):
                go(ring_ag(t, i, x))
            return
        for d in (0, 2, 1):
            go(ag_copy(t, d, x))

    def s4(t):
        h, nh, r0, n, mine, theirs = geometry(t)
        await_all(y.at[pl.ds(h, nh), pl.ds(mine, n // 8 * (1 if t in RING else 3))], ag_r.at[t])
        go(f_copy(t, mine))

    def s5(t):
        h, nh, r0, n, mine, theirs = geometry(t)
        f_copy(t, theirs).wait_recv()

    def z1_arrive(k):
        for d in range(2):
            z1_copy(k, d).wait_recv()

    def z1_arrive(k):
        for d in range(2):
            z1_copy(k, d).wait_recv()

    s1(0)
    h_arrive(0, 0)
    s2(0)
    h_arrive(0, 1)
    h_arrive(0, 2)
    h_arrive(0, 3)
    s3(0)
    s1(1)
    z1_arrive(0)
    z1_arrive(1)
    s1(2)
    h_arrive(1, 0)
    s2(1)
    h_arrive(1, 1)
    s2(2)
    h_arrive(1, 2)
    s4(0)
    z1_arrive(2)
    s1(3)
    h_arrive(1, 3)
    s1(4)
    z1_arrive(3)
    s1(5)
    h_arrive(2, 0)
    s2(4)
    s2(3)
    h_arrive(2, 1)
    s2(5)
    h_arrive(2, 2)
    z2_start((0, 1, 2, 3,))
    s3(1)
    s3(2)
    h_arrive(2, 3)
    s1(6)
    s6(4)
    h_last(0)
    s2(6)
    s6(5)
    h_last(1)
    s1(7)
    z2_arrive(0, (0,))
    s3(3)
    s3(4)
    s2(7)
    z2_arrive(0, (1,))
    s3(5)
    z2_arrive(0, (2,))
    s3(6)
    z2_arrive(0, (3,))
    s4(1)
    s4(2)
    z2_arrive(1, (0,))
    s7(4)
    s7(5)
    s3(7)
    z2_arrive(1, (1,))
    z2_arrive(1, (2,))
    z2_arrive(1, (3,))
    s4(6)
    z2_arrive(2, (0,))
    z2_arrive(2, (1,))
    s4(3)
    s4(4)
    s4(5)
    s4(7)
    z2_arrive(2, (2,))
    z2_arrive(2, (3,))
    z2_arrive(3, (0,))
    z2_arrive(3, (1,))
    s5(0)
    s5(1)
    s5(2)
    s5(3)
    s5(4)
    s5(5)
    s5(6)
    s5(7)

    def block_of(d):
        t = lax.rem(y_pos + d + 8, 8)
        return (d % 2) * 4 + t // 2

    def c_chunk(j):
        rows = pl.ds(j * 256, 256)
        left = jnp.concatenate([z2[s, rows] for s in range(8)], axis=1)
        for q in range(4):
            right = jnp.concatenate([y[2 * q], y[2 * q + 1]], axis=1)
            part = jnp.dot(left, right, preferred_element_type=F32)
            for b in range(2):
                cpart[q * 2 + b, rows] = part[:, b * 128:(b + 1) * 128]

    def c_copy(d, t, j):
        start, size = j * 256, 256
        if t in (0, 1, 4):
            start, size = start + (1 - d if t == 4 else d) * 128, 128
        slot = 1 if t == 4 else t
        return rcopy(
            csend.at[d, slot, pl.ds(start, size)], crecv.at[d, slot, pl.ds(start, size)],
            cs.at[0], cr.at[t, j], ydev[d],
        )

    def c_start(j):
        for d in range(2):
            for t, half in ((0, d), (4, 1 - d)):
                rows = pl.ds(j * 256 + half * 128, 128)
                hop = 4 if t == 0 else 3
                csend[d, t // 4, rows] = cpart[block_of(hop * (1 - 2 * d)), rows].astype(BF)
                go(c_copy(d, t, j))

    def c_wait(t, j):
        await_all(crecv.at[0, 0, pl.ds(0, 512 if t in (2, 3) else 256)], cr.at[t, j])

    def c_step(t, j):
        c_wait(t - 1, j)
        if t == 2:
            c_wait(4, j)
        for d in range(2):
            b = block_of((4 - t) * (1 - 2 * d))
            rows = pl.ds(j * 256 + d * 128, 128) if t == 1 else pl.ds(j * 256, 256)
            csend[d, t, rows] = (cpart[b, rows] + crecv[d, t - 1, rows].astype(F32)).astype(BF)
            go(c_copy(d, t, j))

    stores = []

    def c_last(j):
        full = pl.ds(j * 256, 256)
        v = cpart[block_of(0), full]
        c_wait(3, j)
        for d in range(2):
            v = v + crecv[d, 3, full].astype(F32)
        o_ref[full, :] = v.astype(BF)
        cp = pltpu.make_async_copy(o_ref.at[full], o_hbm.at[full], oo.at[j])
        cp.start()
        stores.append(cp)

    c_chunk(0)
    c_start(0)
    c_chunk(1)
    c_start(1)
    z2_arrive(3, (2,))
    c_chunk(2)
    c_start(2)
    z2_arrive(3, (3,))
    c_chunk(3)
    c_start(3)
    c_step(1, 0)
    c_step(1, 1)
    c_step(1, 2)
    c_step(1, 3)
    c_step(2, 0)
    c_step(2, 1)
    c_step(2, 2)
    c_step(2, 3)
    c_step(3, 0)
    c_step(3, 1)
    c_step(3, 2)
    c_step(3, 3)
    c_last(0)
    c_last(1)
    c_last(2)
    c_last(3)
    for cp in stores:
        cp.wait()
    await_all(ht.at[pl.ds(0, 896)], hs.at[0])
    await_all(z1.at[pl.ds(0, 4)], z1s.at[0])
    await_all(z2.at[pl.ds(0, 7)], z2s.at[0])
    await_all(pbuf.at[:, pl.ds(0, 512)], ks.at[0])
    await_all(rss.at[:, pl.ds(0, 384)], rs_s.at[0])
    await_all(y.at[:, pl.ds(0, 384)], ag_s.at[0])
    await_all(y.at[:, pl.ds(0, 512)], fs.at[0])
    await_all(z2.at[pl.ds(0, 7)], cs.at[0])


def local(hamiltonian, inv_root, h_pattern, z_pattern):
    dma = pltpu.SemaphoreType.DMA
    smem = pl.BlockSpec(memory_space=pltpu.SMEM)
    hbm = pl.BlockSpec(memory_space=pl.ANY)
    return pl.pallas_call(
        body,
        out_shape=jax.ShapeDtypeStruct((1024, 128), BF),
        in_specs=[smem, smem, hbm, hbm],
        out_specs=hbm,
        scratch_shapes=[
            pltpu.VMEM((1024, 128), BF),
            pltpu.VMEM((1024, 512), BF),
            pltpu.VMEM((1024, 128), BF),
            pltpu.VMEM((1024, 1024), BF),
            pltpu.VMEM((8, 1024, 128), BF),
            pltpu.VMEM((8, 1024, 128), BF),
            pltpu.VMEM((8, 1024, 128), BF),
            pltpu.VMEM((8, 1024, 128), F32),
            pltpu.VMEM((8, 1024, 128), F32),
            pltpu.VMEM((8, 1024, 128), BF),
            pltpu.VMEM((3, 8, 1024, 128), BF),
            pltpu.VMEM((8, 1024, 128), F32),
            pltpu.VMEM((2, 4, 1024, 128), BF),
            pltpu.VMEM((2, 4, 1024, 128), BF),
            dma((2,)), dma((4,)),
            dma((1,)), dma((4, 4)),
            dma((1,)), dma((4, 2)),
            dma((1,)), dma((4, 4)),
            dma((1,)), dma((8,)),
            dma((1,)), dma((14,)),
            dma((1,)), dma((14,)),
            dma((1,)), dma((8,)),
            dma((1,)), dma((5, 4)),
        ],
        compiler_params=pltpu.CompilerParams(
            collective_id=0, has_side_effects=True, vmem_limit_bytes=56 * 2**20
        ),
        cost_estimate=pl.CostEstimate(flops=4 * 1024**3, bytes_accessed=3 * 2**19, transcendentals=0),
    )(h_pattern, z_pattern, hamiltonian, inv_root)


def solution(mesh):
    return jax.shard_map(
        local,
        mesh=mesh,
        in_specs=(P("row", ("col", "layer")), P("row", "col"), P(), P()),
        out_specs=P("row", ("col", "layer")),
        check_vma=False,
    )
```

```python
import functools
import jax
import jax.numpy as jnp
from jax import lax
from jax.experimental import pallas as pl
from jax.experimental.pallas import tpu as pltpu
from jax.sharding import PartitionSpec as P

BS = 256
BF = jnp.bfloat16
F32 = jnp.float32
MESH = pl.DeviceIdType.MESH

SRC = ((0, 1, 3, 5), (0, 2, 4, 6))
DST = ((1, 3, 5, 7), (2, 4, 6, 7))

TASKS = (
    (0, 128, 0, 4), (128, 256, 0, 4), (0, 384, 4, 2), (0, 384, 6, 1),
    (384, 256, 0, 7), (0, 640, 7, 1), (640, 256, 0, 8), (896, 128, 0, 8),
)

RING = (4, 5)


def body(hp, zp, h_hbm, z_hbm, o_hbm, h_ref, z_ref, o_ref, ht, z1, z2, y, pbuf, xbuf, rss, rsr, cpart, csend, crecv,
         io, oo, hs, hr, z1s, z1r, z2s, z2r, ks, kr, rs_s, rs_r, ag_s, ag_r, fs, fr, cs, cr):
    row = lax.axis_index("row")
    col = lax.axis_index("col")
    layer = lax.axis_index("layer")
    x, c = row // 2, lax.rem(row, 2)
    y_lo, z = col // 8, lax.rem(col, 8)
    y_pos = layer * 2 + y_lo

    def at_z(d):
        return {"col": y_lo * 8 + lax.rem(z + d + 8, 8)}

    def at_y(d):
        t = lax.rem(y_pos + d + 8, 8)
        return {"col": lax.rem(t, 2) * 8 + z, "layer": t // 2}

    def at_x(d):
        return {"row": lax.rem(x + d + 4, 4) * 2 + c}

    zdev = (at_z(1), at_z(-1))
    ydev = (at_y(1), at_y(-1))
    xdev = (at_x(1), at_x(2), at_x(3))
    sib = {"row": x * 2 + 1 - c}

    loads = [pltpu.make_async_copy(h_hbm, h_ref, io.at[0]), pltpu.make_async_copy(z_hbm, z_ref, io.at[1])]
    for cp in loads:
        cp.start()
    barrier = pltpu.get_barrier_semaphore()
    for d in (*zdev, *ydev, *xdev, sib):
        pl.semaphore_signal(barrier, inc=1, device_id=d, device_id_type=MESH)

    def rcopy(src, dst, s, r, dev):
        return pltpu.make_async_remote_copy(
            src_ref=src, dst_ref=dst, send_sem=s, recv_sem=r, device_id=dev, device_id_type=MESH
        )

    def await_all(ref, sem):
        pltpu.make_async_copy(ref, ref, sem).wait()

    def go(cp):
        cp.start()

    loads[0].wait()
    for i in range(4):
        p = hp[row * 4 + i, col * 2 + layer // 2]
        keep = jnp.where(p > 0, 1.0, 0.0).astype(F32)
        blk = h_ref[i * BS:(i + 1) * BS, :].astype(F32) * keep
        ht[0:128, i * BS:(i + 1) * BS] = blk.T.astype(BF)

    pl.semaphore_wait(barrier, 8)

    def h_copy(d, s, j):
        k, j = j, j if d == 0 else 3 - j
        return rcopy(
            ht.at[pl.ds(SRC[d][s] * 128 + j * 32, 32)], ht.at[pl.ds(DST[d][s] * 128 + j * 32, 32)],
            hs.at[0], hr.at[s, k], zdev[d],
        )

    for j in range(4):
        for d in range(2):
            go(h_copy(d, 0, j))

    def z1_copy(k, d):
        rows = pl.ds(d * 512, 512)
        return rcopy(z1.at[k, rows], z1.at[4 + k, rows], z1s.at[0], z1r.at[k, d], ydev[d])

    loads[1].wait()
    for k in range(2):
        for i in range(4):
            p = zp[row * 4 + i, col * 2 + k]
            keep = jnp.where(p > 0, 1.0, 0.0).astype(F32)
            blk = z_ref[i * BS:(i + 1) * BS, k * BS:(k + 1) * BS].astype(F32) * keep
            for m in range(2):
                z1[2 * k + m, i * BS:(i + 1) * BS, :] = blk[:, m * 128:(m + 1) * 128].astype(BF)
        for m in range(2):
            for d in range(2):
                go(z1_copy(2 * k + m, d))
    z2[0] = z1[layer]

    def z2_copy(d, s, j):
        start, size = j * 256, 256
        if s == 3:
            start, size = start + d * 128, 128
        return rcopy(
            z2.at[SRC[d][s], pl.ds(start, size)], z2.at[DST[d][s], pl.ds(start, size)],
            z2s.at[0], z2r.at[s, j], zdev[d],
        )

    def h_arrive(s, j):
        await_all(ht.at[pl.ds(0, 64)], hr.at[s, j])
        for d in range(2):
            if s < 2 or (s == 2 and j < 2):
                go(h_copy(d, s + 1, j))

    def h_last(j):
        await_all(ht.at[pl.ds(0, 64)], hr.at[3, j])

    def z2_start(js):
        for j in js:
            for d in range(2):
                go(z2_copy(d, 0, j))

    def z2_arrive(s, js):
        for j in js:
            await_all(z2.at[0, pl.ds(0, 256 if s == 3 else 512)], z2r.at[s, j])
            for d in range(2):
                if s < 3:
                    go(z2_copy(d, s + 1, j))

    def geometry(t):
        r0, n, h, nh = TASKS[t]
        mine = pl.multiple_of(r0 + c * (n // 2), 16)
        theirs = pl.multiple_of(r0 + (1 - c) * (n // 2), 16)
        return h, nh, r0, n, mine, theirs

    def quarter(t, q):
        h, nh, r0, n, mine, theirs = geometry(t)
        return pl.multiple_of(mine + q * (n // 8), 16), n // 8

    def s1(t):
        h, nh, r0, n, mine, theirs = geometry(t)
        for k in range(0, nh, 2):
            w = min(2, nh - k)
            right = z1[h + k] if w == 1 else jnp.concatenate([z1[h + k], z1[h + k + 1]], axis=1)
            part = jnp.dot(ht[r0:r0 + n, :], right, preferred_element_type=F32)
            for m in range(w):
                pbuf[h + k + m, r0:r0 + n] = part[:, m * 128:(m + 1) * 128]
        go(k_copy(t, theirs))

    def k_copy(t, start):
        h, nh, r0, n, mine, theirs = geometry(t)
        return rcopy(
            pbuf.at[pl.ds(h, nh), pl.ds(start, n // 2)], xbuf.at[pl.ds(h, nh), pl.ds(start, n // 2)],
            ks.at[0], kr.at[t], sib,
        )

    def rs_copy(t, d, q):
        h, nh = TASKS[t][2:]
        start, size = quarter(t, q)
        return rcopy(
            rss.at[pl.ds(h, nh), pl.ds(start, size)], rsr.at[d, pl.ds(h, nh), pl.ds(start, size)],
            rs_s.at[0], rs_r.at[t], xdev[d],
        )

    def ag_copy(t, d, q):
        h, nh = TASKS[t][2:]
        start, size = quarter(t, q)
        part = y.at[pl.ds(h, nh), pl.ds(start, size)]
        return rcopy(part, part, ag_s.at[0], ag_r.at[t], xdev[d])

    def f_copy(t, start):
        h, nh, r0, n, mine, theirs = geometry(t)
        part = y.at[pl.ds(h, nh), pl.ds(start, n // 2)]
        return rcopy(part, part, fs.at[0], fr.at[t], sib)

    def s2(t):
        h, nh, r0, n, mine, theirs = geometry(t)
        k_copy(t, mine).wait_recv()
        for k in range(nh):
            v = pbuf[h + k, pl.ds(mine, n // 2)] + xbuf[h + k, pl.ds(mine, n // 2)]
            pbuf[h + k, pl.ds(mine, n // 2)] = v
            rss[h + k, pl.ds(mine, n // 2)] = v.astype(BF)
        if t in RING:
            for i in (0, 3, 1, 4):
                go(ring_rs(t, i, x + 2 if i % 3 == 0 else x + sign(i)))
            return
        for d in (0, 2, 1):
            go(rs_copy(t, d, lax.rem(x + d + 1, 4)))

    def sign(i):
        return 1 if i < 3 else -1

    def half_rows(t, q, second):
        start, size = quarter(t, lax.rem(q + 4, 4))
        low = size // 32 * 16
        return pl.ds(start + low, size - low) if second else pl.ds(start, low)

    def ring_rs(t, i, q):
        h, nh = TASKS[t][2:]
        rows = half_rows(t, q, (i % 3 == 1) == (i < 3))
        d = 0 if i < 3 else 2
        return rcopy(
            rss.at[pl.ds(h, nh), rows], rsr.at[d, pl.ds(h, nh), rows], rs_s.at[0], rs_r.at[8 + t if i % 3 == 0 else t], xdev[d]
        )

    def s6(t):
        h, nh = TASKS[t][2:]
        await_all(rsr.at[0, pl.ds(h, nh), pl.ds(*quarter(t, x))], rs_r.at[8 + t])
        for i in (0, 3):
            q = x + sign(i)
            rows = half_rows(t, q, i == 3)
            for k in range(nh):
                v = pbuf[h + k, rows] + rsr[0 if i == 0 else 2, h + k, rows].astype(F32)
                rss[h + k, rows] = v.astype(BF)
            go(ring_rs(t, i + 2, q))

    def ring_ag(t, i, q):
        h, nh = TASKS[t][2:]
        start, size = quarter(t, lax.rem(q + 4, 4))
        rows = pl.ds(start, size) if i < 2 else half_rows(t, q, i == 3)
        part = y.at[pl.ds(h, nh), rows]
        return rcopy(part, part, ag_s.at[0], ag_r.at[8 + t if i < 2 else t], xdev[i % 2 * 2])

    def s7(t):
        h, nh, r0, n, mine, theirs = geometry(t)
        await_all(y.at[pl.ds(h, nh), pl.ds(mine, n // 4)], ag_r.at[8 + t])
        go(ring_ag(t, 2, x - 1))
        go(ring_ag(t, 3, x + 1))

    def s3(t):
        h, nh = TASKS[t][2:]
        start, size = quarter(t, x)
        await_all(rsr.at[pl.ds(0, 2 if t in RING else 3), pl.ds(h, nh), pl.ds(start, size)], rs_r.at[t])
        for k in range(nh):
            v = pbuf[h + k, pl.ds(start, size)]
            for d in (0, 2) if t in RING else (0, 1, 2):
                v = v + rsr[d, h + k, pl.ds(start, size)].astype(F32)
            y[h + k, pl.ds(start, size)] = v.astype(BF)
        if t in RING:
            for i in range(2):
                go(ring_ag(t, i, x))
            return
        for d in (0, 2, 1):
            go(ag_copy(t, d, x))

    def s4(t):
        h, nh, r0, n, mine, theirs = geometry(t)
        await_all(y.at[pl.ds(h, nh), pl.ds(mine, n // 8 * (1 if t in RING else 3))], ag_r.at[t])
        go(f_copy(t, mine))

    def s5(t):
        h, nh, r0, n, mine, theirs = geometry(t)
        f_copy(t, theirs).wait_recv()

    def z1_arrive(k):
        for d in range(2):
            z1_copy(k, d).wait_recv()

    def z1_arrive(k):
        for d in range(2):
            z1_copy(k, d).wait_recv()

    s1(0)
    h_arrive(0, 0)
    s2(0)
    h_arrive(0, 1)
    h_arrive(0, 2)
    h_arrive(0, 3)
    s3(0)
    s1(1)
    z1_arrive(0)
    z1_arrive(1)
    s1(2)
    h_arrive(1, 0)
    s2(1)
    h_arrive(1, 1)
    s2(2)
    h_arrive(1, 2)
    s4(0)
    z1_arrive(2)
    s1(3)
    h_arrive(1, 3)
    s1(4)
    z1_arrive(3)
    s1(5)
    h_arrive(2, 0)
    s2(4)
    s2(3)
    h_arrive(2, 1)
    z2_start((0, 1, 2, 3,))
    s2(5)
    h_arrive(2, 2)
    s3(1)
    s3(2)
    h_arrive(2, 3)
    s1(6)
    s6(4)
    h_last(0)
    s2(6)
    s6(5)
    h_last(1)
    s1(7)
    z2_arrive(0, (0,))
    s3(3)
    s3(4)
    s2(7)
    z2_arrive(0, (1,))
    s3(5)
    z2_arrive(0, (2,))
    s3(6)
    z2_arrive(0, (3,))
    s4(1)
    s4(2)
    z2_arrive(1, (0,))
    s7(4)
    s7(5)
    s3(7)
    z2_arrive(1, (1,))
    z2_arrive(1, (2,))
    z2_arrive(1, (3,))
    s4(6)
    z2_arrive(2, (0,))
    z2_arrive(2, (1,))
    s4(3)
    s4(4)
    s4(5)
    s4(7)
    z2_arrive(2, (2,))
    z2_arrive(2, (3,))
    z2_arrive(3, (0,))
    z2_arrive(3, (1,))
    s5(0)
    s5(1)
    s5(2)
    s5(3)
    s5(4)
    s5(5)
    s5(6)
    s5(7)

    def block_of(d):
        t = lax.rem(y_pos + d + 8, 8)
        return (d % 2) * 4 + t // 2

    def c_chunk(j):
        rows = pl.ds(j * 256, 256)
        left = jnp.concatenate([z2[s, rows] for s in range(8)], axis=1)
        for q in range(4):
            right = jnp.concatenate([y[2 * q], y[2 * q + 1]], axis=1)
            part = jnp.dot(left, right, preferred_element_type=F32)
            for b in range(2):
                cpart[q * 2 + b, rows] = part[:, b * 128:(b + 1) * 128]

    def c_copy(d, t, j):
        start, size = j * 256, 256
        if t in (0, 1, 4):
            start, size = start + (1 - d if t == 4 else d) * 128, 128
        slot = 1 if t == 4 else t
        return rcopy(
            csend.at[d, slot, pl.ds(start, size)], crecv.at[d, slot, pl.ds(start, size)],
            cs.at[0], cr.at[t, j], ydev[d],
        )

    def c_start(j):
        for d in range(2):
            for t, half in ((0, d), (4, 1 - d)):
                rows = pl.ds(j * 256 + half * 128, 128)
                hop = 4 if t == 0 else 3
                csend[d, t // 4, rows] = cpart[block_of(hop * (1 - 2 * d)), rows].astype(BF)
                go(c_copy(d, t, j))

    def c_wait(t, j):
        await_all(crecv.at[0, 0, pl.ds(0, 512 if t in (2, 3) else 256)], cr.at[t, j])

    def c_step(t, j):
        c_wait(t - 1, j)
        if t == 2:
            c_wait(4, j)
        for d in range(2):
            b = block_of((4 - t) * (1 - 2 * d))
            rows = pl.ds(j * 256 + d * 128, 128) if t == 1 else pl.ds(j * 256, 256)
            csend[d, t, rows] = (cpart[b, rows] + crecv[d, t - 1, rows].astype(F32)).astype(BF)
            go(c_copy(d, t, j))

    stores = []

    def c_last(j):
        full = pl.ds(j * 256, 256)
        v = cpart[block_of(0), full]
        c_wait(3, j)
        for d in range(2):
            v = v + crecv[d, 3, full].astype(F32)
        o_ref[full, :] = v.astype(BF)
        cp = pltpu.make_async_copy(o_ref.at[full], o_hbm.at[full], oo.at[j])
        cp.start()
        stores.append(cp)

    c_chunk(0)
    c_start(0)
    c_chunk(1)
    c_start(1)
    z2_arrive(3, (2,))
    c_chunk(2)
    c_start(2)
    z2_arrive(3, (3,))
    c_chunk(3)
    c_start(3)
    c_step(1, 0)
    c_step(1, 1)
    c_step(1, 2)
    c_step(1, 3)
    c_step(2, 0)
    c_step(2, 1)
    c_step(2, 2)
    c_step(2, 3)
    c_step(3, 0)
    c_step(3, 1)
    c_step(3, 2)
    c_step(3, 3)
    c_last(0)
    c_last(1)
    c_last(2)
    c_last(3)
    for cp in stores:
        cp.wait()
    await_all(ht.at[pl.ds(0, 896)], hs.at[0])
    await_all(z1.at[pl.ds(0, 4)], z1s.at[0])
    await_all(z2.at[pl.ds(0, 7)], z2s.at[0])
    await_all(pbuf.at[:, pl.ds(0, 512)], ks.at[0])
    await_all(rss.at[:, pl.ds(0, 384)], rs_s.at[0])
    await_all(y.at[:, pl.ds(0, 384)], ag_s.at[0])
    await_all(y.at[:, pl.ds(0, 512)], fs.at[0])
    await_all(z2.at[pl.ds(0, 7)], cs.at[0])


def local(hamiltonian, inv_root, h_pattern, z_pattern):
    dma = pltpu.SemaphoreType.DMA
    smem = pl.BlockSpec(memory_space=pltpu.SMEM)
    hbm = pl.BlockSpec(memory_space=pl.ANY)
    return pl.pallas_call(
        body,
        out_shape=jax.ShapeDtypeStruct((1024, 128), BF),
        in_specs=[smem, smem, hbm, hbm],
        out_specs=hbm,
        scratch_shapes=[
            pltpu.VMEM((1024, 128), BF),
            pltpu.VMEM((1024, 512), BF),
            pltpu.VMEM((1024, 128), BF),
            pltpu.VMEM((1024, 1024), BF),
            pltpu.VMEM((8, 1024, 128), BF),
            pltpu.VMEM((8, 1024, 128), BF),
            pltpu.VMEM((8, 1024, 128), BF),
            pltpu.VMEM((8, 1024, 128), F32),
            pltpu.VMEM((8, 1024, 128), F32),
            pltpu.VMEM((8, 1024, 128), BF),
            pltpu.VMEM((3, 8, 1024, 128), BF),
            pltpu.VMEM((8, 1024, 128), F32),
            pltpu.VMEM((2, 4, 1024, 128), BF),
            pltpu.VMEM((2, 4, 1024, 128), BF),
            dma((2,)), dma((4,)),
            dma((1,)), dma((4, 4)),
            dma((1,)), dma((4, 2)),
            dma((1,)), dma((4, 4)),
            dma((1,)), dma((8,)),
            dma((1,)), dma((14,)),
            dma((1,)), dma((14,)),
            dma((1,)), dma((8,)),
            dma((1,)), dma((5, 4)),
        ],
        compiler_params=pltpu.CompilerParams(
            collective_id=0, has_side_effects=True, vmem_limit_bytes=56 * 2**20
        ),
        cost_estimate=pl.CostEstimate(flops=4 * 1024**3, bytes_accessed=3 * 2**19, transcendentals=0),
    )(h_pattern, z_pattern, hamiltonian, inv_root)


def solution(mesh):
    return jax.shard_map(
        local,
        mesh=mesh,
        in_specs=(P("row", ("col", "layer")), P("row", "col"), P(), P()),
        out_specs=P("row", ("col", "layer")),
        check_vma=False,
    )
```
